128 devices in a mesh: pipe: 8 (over x, y_lo), dp: 16 (over y_hi, z, core).
Axes of the slice: x: 4, y: 4 (y_hi: 2, y_lo: 2; y = y_hi * 2 + y_lo), z: 4, core: 2. Of those that a mesh axis runs over, the one named last changes fastest.
Arguments:
- section_output: bfloat16 [2048, 4608], P('dp', 'pipe'), may hold values from -0.29882812 to 0.29882812
- norm_gain: bfloat16 [4608], P('pipe'), may hold values from 0.5 to 1.5
- head_weight: bfloat16 [65536, 4608], P(('pipe', 'dp')), may hold values from -0.25 to 0.25
- targets: int32 [2048], replicated, may hold values from 0 to 65535
Outputs:
- token_loss: float32 [2048], P('dp')
- grad_input: bfloat16 [2048, 4608], P('dp', 'pipe')
- head_grad: bfloat16 [65536, 4608], P(('pipe', 'dp'))
- gain_grad: float32 [4608], P('pipe')
The draws below stay inside these ranges and needn't reach their ends.
All inputs are finite; a program needn't handle non-finite values.
Results may differ from the reference program's by a relative error of at most 0.017.
Values may be sent and summed in bfloat16 or wider, within the bound.
No kernel may reach another device: no remote copies, remote signals or barrier semaphores. Data moves between devices by JAX's collectives and lax.ppermute only.
A program may use at most 128 MiB of HBM per device.

```python
import jax
import jax.numpy as jnp
from jax import lax

D = 4608
V_DEV = 512
TOKENS = 2048
VOCAB = 65536


def with_ends(drawn, stream_key, smallest, high):
    shape = drawn.shape
    index_at = [jax.random.randint(jax.random.fold_in(stream_key, axis), (), 0, shape[axis]) for axis in range(len(shape))]
    drawn = drawn.at[tuple(index_at)].set(smallest)
    longest = shape.index(max(shape))
    index_at[longest] = (index_at[longest] + 1) % shape[longest]
    return drawn.at[tuple(index_at)].set(high)


def block_scale(own_key, extent, cuts, least, top_value):
    def one(dim, blocks):
        draws = jax.random.uniform(jax.random.fold_in(jax.random.fold_in(own_key, 6), dim), (blocks,), jnp.float32, least / len(cuts), top_value / len(cuts))
        return jnp.repeat(jnp.exp(draws), extent[dim] // blocks).reshape((-1,) + (1,) * (len(extent) - dim - 1))

    factor_of = one(*cuts[0])
    for cut in cuts[1:]:
        factor_of = factor_of * one(*cut)
    return factor_of


def bell_draw(key, dims, spread, most, shards=(), kind=jnp.bfloat16):
    values = spread * jax.random.normal(key, dims, jnp.float32)
    if shards:
        values = values * block_scale(key, dims, shards, -0.22, 0.18)
    return jnp.clip(values, -most, most).astype(kind)


def setup_inputs(seed: int = 0) -> dict:
    seeds = jax.random.split(jax.random.key(seed), 5)
    section_output = bell_draw(seeds[0], (TOKENS, D), 0.05, 0.29882812, ((0, 16), (1, 8)))
    norm_gain = jnp.clip(1.0 + 0.1 * jax.random.normal(seeds[1], (D,), jnp.float32), 0.5, 1.5).astype(jnp.bfloat16)
    head_weight = bell_draw(seeds[2], (VOCAB, D), (D // 9) ** -0.5, 0.25, ((0, 128),))
    targets = with_ends(jax.random.randint(seeds[3], (TOKENS,), 0, VOCAB), jax.random.fold_in(seeds[3], 1), 0, VOCAB - 1).astype(jnp.int32)
    return {"section_output": section_output, "norm_gain": norm_gain, "head_weight": head_weight, "targets": targets}


CAP = 30.0
EPS = 1e-06

def reference(section_output, norm_gain, head_weight, targets):
    xf = section_output.astype(jnp.float32)
    rinv = lax.rsqrt(lax.optimization_barrier(jnp.mean(xf * xf, axis=1, keepdims=True)) + EPS)
    gain = norm_gain.astype(jnp.float32)
    hidden = (xf * rinv * gain).astype(jnp.bfloat16)
    nblk = head_weight.shape[0] // V_DEV
    blocks = head_weight.reshape(nblk, V_DEV, D)
    bases = jnp.arange(nblk, dtype=jnp.int32) * V_DEV

    def capped_of(block):
        act = jnp.dot(hidden, block.T, preferred_element_type=jnp.float32)
        tv = jnp.tanh(act / CAP)
        return (CAP * tv, tv)

    def stats(carry, inputs):
        block, base = inputs
        capped, tv = capped_of(block)
        cols = base + jnp.arange(V_DEV, dtype=jnp.int32)
        hits = targets[:, None] == cols[None, :]
        return ((carry[0] + lax.optimization_barrier(jnp.sum(jnp.exp(capped), 1)), carry[1] + lax.optimization_barrier(jnp.sum(jnp.where(hits, capped, 0.0), 1))), None)
    zeros = jnp.zeros((section_output.shape[0],), jnp.float32)
    (total, picked), unused = lax.scan(stats, (zeros, zeros), (blocks, bases))
    token_loss = jnp.log(total) - picked

    def backward(carry, inputs):
        block, base = inputs
        capped, tv = capped_of(block)
        cols = base + jnp.arange(V_DEV, dtype=jnp.int32)
        hits = (targets[:, None] == cols[None, :]).astype(jnp.float32)
        grad_act = ((jnp.exp(capped) / total[:, None] - hits) * (1.0 - tv * tv)).astype(jnp.bfloat16)
        block_grad = jnp.dot(grad_act.T, hidden, preferred_element_type=jnp.float32).astype(jnp.bfloat16)
        term = jnp.dot(grad_act, block, preferred_element_type=jnp.float32).astype(jnp.bfloat16)
        return (carry + term.astype(jnp.float32), block_grad)
    start = jnp.zeros((section_output.shape[0], D), jnp.float32)
    grad_hidden, grads = lax.scan(backward, start, (blocks, bases))
    head_grad = grads.reshape(nblk * V_DEV, D)
    scaled = grad_hidden * gain
    inner = lax.optimization_barrier(jnp.sum(scaled * xf, axis=1, keepdims=True))
    grad_input = (rinv * scaled - xf * rinv ** 3 * inner / D).astype(jnp.bfloat16)
    gain_grad = lax.optimization_barrier(jnp.sum(grad_hidden * xf * rinv, axis=0))
    return (token_loss, grad_input, head_grad, gain_grad)
```

```python
import functools

import jax
import jax.numpy as jnp
import numpy as np
from jax import lax
from jax.experimental import pallas as pl
from jax.experimental.pallas import tpu as pltpu
from jax.sharding import Mesh, PartitionSpec as P

AX = ("x", "ylo", "yhi", "z", "core")
D = 4608
FB = 576
PT = 192
SQ = 16
TB = 128
VB = 512
CAP = 30.0
EPS = 1e-06
VMEM = 60 * 1024 * 1024
BF = jnp.bfloat16
F32 = jnp.float32

ORDER = ((0, 1, 2), (1, 2, 0), (2, 0, 1))


def coords(i):
    core, z, yhi, ylo, x = i % 2, i // 2 % 4, i // 8 % 2, i // 16 % 2, i // 32
    return [x, yhi * 2 + ylo, z], core


def number(c, core):
    return (((c[0] * 2 + c[1] % 2) * 2 + c[1] // 2) * 4 + c[2]) * 2 + core


@functools.cache
def ring(dim, k):
    pairs = []
    for i in range(128):
        c, core = coords(i)
        c[dim] = (c[dim] + (k if core == 0 else -k)) % 4
        pairs.append((i, number(c, core)))
    return pairs


@functools.cache
def twin():
    return [(i, i ^ 1) for i in range(128)]


@functools.cache
def offset(dy, dz):
    pairs = []
    for i in range(128):
        c, core = coords(i)
        c[1], c[2] = (c[1] + dy) % 4, (c[2] + dz) % 4
        pairs.append((i, number(c, core)))
    return pairs


def send(a, pairs):
    return lax.ppermute(a, AX, pairs)


def gather(blocks):
    held = list(blocks)
    got = [[send(held[p], ring(ORDER[p][0], k)) for k in (1, 2, 3)] for p in range(3)]
    held = [jnp.stack([held[p], got[p][2], got[p][1], got[p][0]]) for p in range(3)]
    for phase in (1, 2):
        back = [send(held[p], ring(ORDER[p][phase], 1)) for p in range(3)]
        front = [send(held[p], ring(ORDER[p][phase], 3)) for p in range(3)]
        far = [send(back[p], ring(ORDER[p][phase], 1)) for p in range(3)]
        four = [[held[p], front[p], far[p], back[p]] for p in range(3)]
        if phase == 1:
            held = [jnp.stack(f) for f in four]
    return four


def split3(v):
    hi = lax.reduce_precision(v, 8, 7)
    mid = lax.reduce_precision(v - hi, 8, 7)
    lo = v - hi - mid
    return [hi.astype(BF), mid.astype(BF), lo.astype(BF)]


def flip_kernel(own_ref, other_ref, a_ref, b_ref, c_ref):
    for h, ref in enumerate((own_ref, other_ref)):
        turned = ref[...].T
        cols = pl.ds(h * VB, VB)
        for ylo in range(2):
            at = ylo * FB
            a_ref[0, ylo, :, cols] = turned[at : at + PT]
            b_ref[0, ylo, :, cols] = turned[at + PT : at + 2 * PT]
            c_ref[ylo, 0, :, cols] = turned[at + 2 * PT : at + 3 * PT]


def flip(own, other):
    block = pl.BlockSpec((VB, 2 * FB), lambda x: (0, x))
    return pl.pallas_call(
        flip_kernel,
        grid=(4,),
        in_specs=[block, block],
        out_specs=[
            pl.BlockSpec((1, 2, PT, 2 * VB), lambda x: (x, 0, 0, 0)),
            pl.BlockSpec((1, 2, PT, 2 * VB), lambda x: (x, 0, 0, 0)),
            pl.BlockSpec((2, 1, PT, 2 * VB), lambda x: (0, x, 0, 0)),
        ],
        out_shape=[
            jax.ShapeDtypeStruct((4, 2, PT, 2 * VB), BF),
            jax.ShapeDtypeStruct((4, 2, PT, 2 * VB), BF),
            jax.ShapeDtypeStruct((2, 4, PT, 2 * VB), BF),
        ],
        compiler_params=pltpu.CompilerParams(vmem_limit_bytes=VMEM),
        cost_estimate=pl.CostEstimate(
            flops=0, bytes_accessed=4 * VB * D * 2, transcendentals=0
        ),
        name="flip",
    )(own, other)


def act_kernel(where, *refs):
    parts = [refs[4 * p : 4 * p + 4] for p in range(3)]
    own_ref, other_ref, tgt_ref = refs[12:15]
    tanh_ref, stat_ref, rinv_ref, xt_out = refs[15:19]
    xt, squares, acc, sems, out_sems = refs[19:]
    step = pl.program_id(0)
    here = (where[0], where[1], where[2])
    sign = where[3]
    base = (where[4], where[5])

    @pl.when(step == 0)
    def _():
        for p in range(3):
            for k3 in range(4):
                for k2 in range(4):
                    for k1 in range(4):
                        at = [None, None, None]
                        for phase, k in enumerate((k1, k2, k3)):
                            dim = ORDER[p][phase]
                            at[dim] = (here[dim] + sign * k) & 3
                        x, y, z = at
                        fb = x * 2 + (y & 1)
                        lanes = pl.ds(pl.multiple_of((y >> 1) * TB, TB), TB)
                        src = parts[p][k3].at[k2, k1]
                        pltpu.make_async_copy(
                            src.at[pl.ds(0, PT)],
                            xt.at[z, pl.ds(pl.multiple_of(fb * FB + p * PT, 16), PT), lanes],
                            sems.at[z],
                        ).start()
                        if p == 0:
                            pltpu.make_async_copy(
                                src.at[pl.ds(PT, SQ)],
                                squares.at[z, pl.ds(pl.multiple_of(fb * SQ, 16), SQ), lanes],
                                sems.at[z],
                            ).start()

    pltpu.make_async_copy(xt.at[step], xt.at[step], sems.at[step]).wait()
    pltpu.make_async_copy(squares.at[step], squares.at[step], sems.at[step]).wait()
    pltpu.make_async_copy(xt.at[step], xt_out.at[step], out_sems.at[step]).start()
    mean = jnp.sum(squares[step].astype(F32), axis=0, keepdims=True) / D
    rinv = lax.rsqrt(mean + EPS)
    rinv_ref[0] = rinv
    tgt = tgt_ref[0]
    rows = 32
    zeros = jnp.zeros((rows, 2 * TB), F32)
    sums = (zeros, zeros, zeros, zeros)
    for h, w_ref in enumerate((own_ref, other_ref)):
        acc[...] = jnp.dot(w_ref[...], xt[step], preferred_element_type=F32)
        row0 = lax.broadcasted_iota(jnp.int32, (rows, 2 * TB), 0) + base[h]

        def chunk(i, sums, h=h, row0=row0):
            total, picked, slope, slope_at = sums
            at = pl.multiple_of(i * rows, rows)
            act = acc[pl.ds(at, rows), :] * rinv
            t = jnp.tanh(act * (1.0 / CAP))
            tanh_ref[0, pl.ds(h * VB + at, rows), :] = t
            expo = jnp.exp(t * CAP)
            bent = (1.0 - t * t) * act
            hit = row0 + at == tgt
            return (
                total + expo,
                picked + jnp.where(hit, t * CAP, 0.0),
                slope + expo * bent,
                slope_at + jnp.where(hit, bent, 0.0),
            )

        sums = lax.fori_loop(0, VB // rows, chunk, sums)
    stat_ref[0] = jnp.concatenate(
        [jnp.sum(s, axis=0, keepdims=True) for s in sums], axis=0
    )
    @pl.when(step == 3)
    def _():
        for z in range(4):
            pltpu.make_async_copy(xt.at[z], xt_out.at[z], out_sems.at[z]).wait()


def act_call(where, parts, own, other, tgt):
    whole = pl.BlockSpec((VB, D), lambda z, w: (0, 0), pipeline_mode=pl.Buffered(1))
    row = pl.BlockSpec((1, 1, 2 * TB), lambda z, w: (z, 0, 0))
    anywhere = pl.BlockSpec(memory_space=pl.ANY)
    return pl.pallas_call(
        act_kernel,
        grid_spec=pltpu.PrefetchScalarGridSpec(
            num_scalar_prefetch=1,
            grid=(4,),
            in_specs=[anywhere] * 12 + [whole, whole, row],
            out_specs=[
                pl.BlockSpec((1, 2 * VB, 2 * TB), lambda z, w: (z, 0, 0)),
                pl.BlockSpec((1, 4, 2 * TB), lambda z, w: (z, 0, 0)),
                row,
                anywhere,
            ],
            scratch_shapes=[
                pltpu.VMEM((4, D, 2 * TB), BF),
                pltpu.VMEM((4, 8 * SQ, 2 * TB), BF),
                pltpu.VMEM((VB, 2 * TB), F32),
                pltpu.SemaphoreType.DMA((4,)),
                pltpu.SemaphoreType.DMA((4,)),
            ],
        ),
        out_shape=[
            jax.ShapeDtypeStruct((4, 2 * VB, 2 * TB), F32),
            jax.ShapeDtypeStruct((4, 4, 2 * TB), F32),
            jax.ShapeDtypeStruct((4, 1, 2 * TB), F32),
            jax.ShapeDtypeStruct((4, D, 2 * TB), BF),
        ],
        compiler_params=pltpu.CompilerParams(vmem_limit_bytes=VMEM),
        cost_estimate=pl.CostEstimate(
            flops=2 * 1024 * 1024 * D, bytes_accessed=30_000_000, transcendentals=2 << 20
        ),
        name="act",
    )(where, *[a for part in parts for a in part], own, other, tgt)


def pieces(where, ks, gz, gy, w0, w1, w2, outs):
    here = (where[0], where[1], where[2])
    sign = where[3]

    def place(dim, at):
        return ((at - here[dim]) * sign) & 3

    for n, k in enumerate(ks):
        out0, out1, out2 = outs[3 * n : 3 * n + 3]
        z = (here[2] + sign * k) & 3
        for x in range(4):
            got = jnp.dot(
                w0[x].reshape(2 * PT, 2 * VB), gz[z], preferred_element_type=F32
            ).astype(BF)
            for ylo in range(2):
                for yhi in range(2):
                    out0[place(1, yhi * 2 + ylo), place(0, x)] = got[
                        ylo * PT : (ylo + 1) * PT, yhi * TB : (yhi + 1) * TB
                    ]
        x = (here[0] + sign * k) & 3
        for z in range(4):
            got = jnp.dot(
                w1[x].reshape(2 * PT, 2 * VB), gz[z], preferred_element_type=F32
            ).astype(BF)
            for ylo in range(2):
                for yhi in range(2):
                    out1[place(2, z), place(1, yhi * 2 + ylo)] = got[
                        ylo * PT : (ylo + 1) * PT, yhi * TB : (yhi + 1) * TB
                    ]
        y = (here[1] + sign * k) & 3
        for zp in range(2):
            got = jnp.dot(
                w2[y & 1].reshape(4 * PT, 2 * VB), gy[y >> 1, zp], preferred_element_type=F32
            ).astype(BF)
            for x in range(4):
                for z in range(2):
                    out2[place(0, x), place(2, 2 * zp + z)] = got[
                        x * PT : (x + 1) * PT, z * TB : (z + 1) * TB
                    ]


def grad_kernel(where, t_ref, total_ref, rinv_ref, tgt_ref, w0, w1, w2, *outs):
    gz, gr, gy = outs[:3]
    base = (where[4], where[5])
    rows = 32

    def chunk(i, carry, z, h, inv, rinv, tgt, row0):
        at = pl.multiple_of(i * rows, rows)
        here = pl.ds(h * VB + at, rows)
        t = t_ref[z, here, :]
        hit = jnp.where(row0 + at == tgt, 1.0, 0.0)
        g = (jnp.exp(t * CAP) * inv - hit) * (1.0 - t * t)
        gr[z, here, :] = (g * rinv).astype(BF)
        g = g.astype(BF)
        gz[z, here, :] = g
        for yhi in range(2):
            gy[yhi, z // 2, here, pl.ds(z % 2 * TB, TB)] = g[:, yhi * TB : (yhi + 1) * TB]
        return carry

    for z in range(4):
        for h in range(2):
            row0 = lax.broadcasted_iota(jnp.int32, (rows, 2 * TB), 0) + base[h]
            lax.fori_loop(
                0,
                VB // rows,
                functools.partial(
                    chunk, z=z, h=h, inv=1.0 / total_ref[z], rinv=rinv_ref[z],
                    tgt=tgt_ref[z], row0=row0,
                ),
                0,
            )
    pieces(where, (2,), gz, gy, w0, w1, w2, outs[3:])


def more_kernel(ks, where, gz, gy, w0, w1, w2, *outs):
    pieces(where, ks, gz, gy, w0, w1, w2, outs)


SMEM_SPEC = pl.BlockSpec(memory_space=pltpu.SMEM)
VMEM_SPEC = pl.BlockSpec(memory_space=pltpu.VMEM)
PIECE = jax.ShapeDtypeStruct((4, 4, PT, TB), BF)


def grad_call(where, t, total, rinv, tgt, turned):
    shapes = [
        jax.ShapeDtypeStruct((4, 2 * VB, 2 * TB), BF),
        jax.ShapeDtypeStruct((4, 2 * VB, 2 * TB), BF),
        jax.ShapeDtypeStruct((2, 2, 2 * VB, 2 * TB), BF),
    ] + [PIECE] * 3
    return pl.pallas_call(
        grad_kernel,
        in_specs=[SMEM_SPEC] + [VMEM_SPEC] * 7,
        out_specs=[VMEM_SPEC] * 6,
        out_shape=shapes,
        compiler_params=pltpu.CompilerParams(vmem_limit_bytes=VMEM),
        cost_estimate=pl.CostEstimate(
            flops=2 * 1024 * 1024 * D // 4, bytes_accessed=24_000_000, transcendentals=1 << 20
        ),
        name="grad",
    )(where, t, total, rinv, tgt, *turned)


def more_call(ks, where, gz, gy, turned):
    return pl.pallas_call(
        functools.partial(more_kernel, ks),
        in_specs=[SMEM_SPEC] + [VMEM_SPEC] * 5,
        out_specs=[VMEM_SPEC] * (3 * len(ks)),
        out_shape=[PIECE] * (3 * len(ks)),
        compiler_params=pltpu.CompilerParams(vmem_limit_bytes=VMEM),
        cost_estimate=pl.CostEstimate(
            flops=2 * 1024 * 1024 * D // 4 * len(ks), bytes_accessed=16_000_000, transcendentals=0
        ),
        name="more%d" % len(ks),
    )(where, gz, gy, *turned)


def head_kernel(gr, xt, own_ref, other_ref):
    for h, ref in enumerate((own_ref, other_ref)):
        total = None
        for z in range(4):
            part = lax.dot_general(
                gr[z, h * VB : (h + 1) * VB, :], xt[z],
                (((1,), (1,)), ((), ())), preferred_element_type=F32,
            )
            total = part if total is None else total + part
        ref[...] = total.astype(BF)


def head_call(gr, xt):
    tile = 512
    return pl.pallas_call(
        head_kernel,
        grid=(D // tile,),
        in_specs=[
            pl.BlockSpec((4, 2 * VB, 2 * TB), lambda f: (0, 0, 0), pipeline_mode=pl.Buffered(1)),
            pl.BlockSpec((4, tile, 2 * TB), lambda f: (0, f, 0)),
        ],
        out_specs=[pl.BlockSpec((VB, tile), lambda f: (0, f))] * 2,
        out_shape=[jax.ShapeDtypeStruct((VB, D), BF)] * 2,
        compiler_params=pltpu.CompilerParams(vmem_limit_bytes=VMEM),
        cost_estimate=pl.CostEstimate(
            flops=2 * 1024 * 1024 * D, bytes_accessed=22_000_000, transcendentals=0
        ),
        name="head",
    )(gr, xt)


def add(a, b):
    return (a.astype(F32) + b.astype(F32)).astype(a.dtype)


def shards(section_output, norm_gain, head_weight, targets):
    x, ylo, yhi, z, core = (lax.axis_index(a) for a in AX)
    y = yhi * 2 + ylo
    shard = (((x * 2 + ylo) * 2 + yhi) * 4 + z) * 2 + core
    where = jnp.stack(
        [x, y, z, 1 - 2 * core, shard * VB, (shard ^ 1) * VB]
    ).astype(jnp.int32)

    other = send(head_weight, twin())

    xt = section_output.T.astype(F32)
    gain = norm_gain.astype(F32)[:, None]
    scaled_x = (xt * gain).astype(BF)
    squares = jnp.sum(xt * xt, axis=0, keepdims=True)
    extra = jnp.concatenate(
        split3(squares) + [jnp.zeros((SQ - 3, TB), BF)], axis=0
    )
    blocks = [
        jnp.concatenate([scaled_x[:PT], extra], axis=0),
        scaled_x[PT : 2 * PT],
        scaled_x[2 * PT :],
    ]
    parts = gather(blocks)
    turned = flip(head_weight, other)

    tgt = lax.dynamic_index_in_dim(
        targets.reshape(2, 4, 2, TB), core, axis=2, keepdims=False
    ).transpose(1, 0, 2).reshape(4, 1, 2 * TB)

    t, stats, rinv, xt_all = act_call(where, parts, head_weight, other, tgt)
    for dim in (2, 1, 0):
        stats = stats + send(stats, ring(dim, 1)) + send(stats, ring(dim, 2)) + send(stats, ring(dim, 3))
    total, picked, slope, slope_at = (stats[:, i : i + 1] for i in range(4))

    out = grad_call(where, t, total, rinv, tgt, turned)
    gz, gr, gy = out[:3]
    far = list(out[3:])
    first = [ORDER[p][2] for p in range(3)]
    got = [send(far[p], ring(first[p], 1)) for p in range(3)]
    near = more_call((1, 3), where, gz, gy, turned)
    up, down = near[:3], near[3:]
    from_front = [send(down[p], ring(first[p], 3)) for p in range(3)]
    from_back = [send(add(up[p], got[p]), ring(first[p], 1)) for p in range(3)]
    mine = more_call((0,), where, gz, gy, turned)
    head_own, head_other = head_call(gr, xt_all)
    head_grad = add(head_own, send(head_other, twin()))

    held = [
        (mine[p].astype(F32) + from_front[p].astype(F32) + from_back[p].astype(F32)).astype(BF)
        for p in range(3)
    ]
    dims = [ORDER[p][1] for p in range(3)]
    got = [send(held[p][2], ring(dims[p], 1)) for p in range(3)]
    from_front = [send(held[p][3], ring(dims[p], 3)) for p in range(3)]
    from_back = [send(add(held[p][1], got[p]), ring(dims[p], 1)) for p in range(3)]
    held = [
        (held[p][0].astype(F32) + from_front[p].astype(F32) + from_back[p].astype(F32)).astype(BF)
        for p in range(3)
    ]
    dims = [ORDER[p][0] for p in range(3)]
    got = [[send(held[p][k], ring(dims[p], k)) for k in (1, 2, 3)] for p in range(3)]
    grad_hidden = jnp.concatenate(
        [held[p][0].astype(F32) + sum(g.astype(F32) for g in got[p]) for p in range(3)], axis=0
    )

    def mine_of(v):
        return lax.dynamic_slice(v, (z, 0, yhi * TB), (1, 1, TB)).reshape(1, TB)

    total, picked, slope, slope_at, rinv = (
        mine_of(v) for v in (total, picked, slope, slope_at, rinv)
    )
    token_loss = (jnp.log(total) - picked).reshape(TB)
    inner = slope / total - slope_at
    grad_input = (rinv * (grad_hidden * gain) - xt * (rinv * rinv * inner / D)).astype(BF).T
    gain_part = jnp.sum(grad_hidden * xt * rinv, axis=1)
    gain_part = gain_part + send(gain_part, twin())
    gain_grad = gain_part + sum(
        send(gain_part, offset(dy, dz)) for dy in (0, 2) for dz in range(4) if dy or dz
    )
    return (token_loss, grad_input, head_grad, gain_grad)


def solution(mesh):
    fine = Mesh(mesh.devices.reshape(4, 2, 2, 4, 2), AX)
    pipe, dp = ("x", "ylo"), ("yhi", "z", "core")
    return jax.shard_map(
        shards,
        mesh=fine,
        in_specs=(P(dp, pipe), P(pipe), P(pipe + dp, None), P()),
        out_specs=(P(dp), P(dp, pipe), P(pipe + dp, None), P(pipe)),
        check_vma=False,
    )
```

```python
import functools

import jax
import jax.numpy as jnp
import numpy as np
from jax import lax
from jax.experimental import pallas as pl
from jax.experimental.pallas import tpu as pltpu
from jax.sharding import Mesh, PartitionSpec as P

AX = ("x", "ylo", "yhi", "z", "core")
D = 4608
FB = 576
PT = 192
SQ = 16
TB = 128
VB = 512
CAP = 30.0
EPS = 1e-06
VMEM = 60 * 1024 * 1024
BF = jnp.bfloat16
F32 = jnp.float32

ORDER = ((0, 1, 2), (1, 2, 0), (2, 0, 1))


def coords(i):
    core, z, yhi, ylo, x = i % 2, i // 2 % 4, i // 8 % 2, i // 16 % 2, i // 32
    return [x, yhi * 2 + ylo, z], core


def number(c, core):
    return (((c[0] * 2 + c[1] % 2) * 2 + c[1] // 2) * 4 + c[2]) * 2 + core


@functools.cache
def across(dim, step):
    pairs = []
    for i in range(128):
        c, core = coords(i)
        bit = step if core == 0 else 1 - step
        gray = (c[dim] ^ (c[dim] >> 1)) ^ (1 << bit)
        c[dim] = gray ^ (gray >> 1)
        pairs.append((i, number(c, core)))
    return pairs


TWIN = [(i, i ^ 1) for i in range(128)]


def send(a, pairs):
    return lax.ppermute(a, AX, pairs)


def gather(blocks):
    held = [b[None] for b in blocks]
    for phase in range(3):
        for step in range(2):
            got = [send(held[p], across(ORDER[p][phase], step)) for p in range(3)]
            if phase == 2 and step == 1:
                return [a for p in range(3) for a in (held[p], got[p])]
            held = [jnp.concatenate([held[p], got[p]]) for p in range(3)]


def reduce_scatter(away, kept):
    for phase in (2, 1, 0):
        for step in (1, 0):
            got = [send(away[p], across(ORDER[p][phase], step)) for p in range(3)]
            if phase == 0 and step == 0:
                return [kept[p][0].astype(F32) + got[p][0].astype(F32) for p in range(3)]
            half = kept[0].shape[0] // 2
            away = [add(kept[p][half:], got[p][half:]) for p in range(3)]
            kept = [add(kept[p][:half], got[p][:half]) for p in range(3)]


def split3(v):
    hi = lax.reduce_precision(v, 8, 7)
    mid = lax.reduce_precision(v - hi, 8, 7)
    lo = v - hi - mid
    return [hi.astype(BF), mid.astype(BF), lo.astype(BF)]


def add(a, b):
    return (a.astype(F32) + b.astype(F32)).astype(a.dtype)


def table(x, y, z, core, shard):
    out = []
    place = jnp.arange(4, dtype=jnp.int32)
    turned = jnp.where(core == 0, place, (place & 1) * 2 + (place >> 1))
    for c in (x, y, z):
        gray = (c ^ (c >> 1)) ^ turned
        out.append(gray ^ (gray >> 1))
    for c in (x, y, z):
        gray = (place ^ (place >> 1)) ^ (c ^ (c >> 1))
        out.append(jnp.where(core == 0, gray, (gray & 1) * 2 + (gray >> 1)))
    out.append(jnp.stack([shard * VB, (shard ^ 1) * VB]))
    return jnp.concatenate(out).astype(jnp.int32)


def at_of(tab, dim, place):
    return tab[4 * dim + place]


def place_of(tab, dim, at):
    return tab[12 + 4 * dim + at]


def flip_kernel(own_ref, other_ref, a_ref, b_ref, c_ref):
    for h, ref in enumerate((own_ref, other_ref)):
        turned = ref[...].T
        cols = pl.ds(h * VB, VB)
        for ylo in range(2):
            at = ylo * FB
            a_ref[0, ylo, :, cols] = turned[at : at + PT]
            b_ref[0, ylo, :, cols] = turned[at + PT : at + 2 * PT]
            c_ref[ylo, 0, :, cols] = turned[at + 2 * PT : at + 3 * PT]


def flip(own, other):
    block = pl.BlockSpec((VB, 2 * FB), lambda x: (0, x))
    return pl.pallas_call(
        flip_kernel,
        grid=(4,),
        in_specs=[block, block],
        out_specs=[
            pl.BlockSpec((1, 2, PT, 2 * VB), lambda x: (x, 0, 0, 0)),
            pl.BlockSpec((1, 2, PT, 2 * VB), lambda x: (x, 0, 0, 0)),
            pl.BlockSpec((2, 1, PT, 2 * VB), lambda x: (0, x, 0, 0)),
        ],
        out_shape=[
            jax.ShapeDtypeStruct((4, 2, PT, 2 * VB), BF),
            jax.ShapeDtypeStruct((4, 2, PT, 2 * VB), BF),
            jax.ShapeDtypeStruct((2, 4, PT, 2 * VB), BF),
        ],
        compiler_params=pltpu.CompilerParams(vmem_limit_bytes=VMEM),
        cost_estimate=pl.CostEstimate(
            flops=0, bytes_accessed=4 * VB * D * 2, transcendentals=0
        ),
        name="flip",
    )(own, other)


def act_kernel(tab, *refs):
    halves = [refs[2 * p : 2 * p + 2] for p in range(3)]
    own_ref, other_ref = refs[6:8]
    act_ref, total_ref, rinv_ref, xt_out = refs[8:12]
    xt, squares, weights, acc, sems, out_sems, w_sems = refs[12:]
    step = pl.program_id(0)

    def fetch(src, tile, x, y, part):
        row = (x * 2 + (y & 1)) * FB + part * PT
        lanes = pl.ds(pl.multiple_of((y >> 1) * TB, TB), TB)
        pltpu.make_async_copy(
            src.at[pl.ds(0, PT)],
            xt.at[tile, pl.ds(pl.multiple_of(row, 16), PT), lanes],
            sems.at[tile],
        ).start()
        if part == 0:
            row = (x * 2 + (y & 1)) * SQ
            pltpu.make_async_copy(
                src.at[pl.ds(PT, SQ)],
                squares.at[tile, pl.ds(pl.multiple_of(row, 16), SQ), lanes],
                sems.at[tile],
            ).start()

    def issue(tile, carry):
        for half in range(2):
            @pl.when((tile >> 1) == half)
            def _():
                for ky in range(4):
                    for kx in range(4):
                        src = halves[0][half].at[((tile & 1) * 4 + ky) * 4 + kx]
                        fetch(src, tile, at_of(tab, 0, kx), at_of(tab, 1, ky), 0)
        for half in range(2):
            for low in range(2):
                for k in range(4):
                    src = halves[1][half].at[(low * 4 + tile) * 4 + k]
                    fetch(src, tile, at_of(tab, 0, half * 2 + low), at_of(tab, 1, k), 1)
                    src = halves[2][half].at[(low * 4 + k) * 4 + tile]
                    fetch(src, tile, at_of(tab, 0, k), at_of(tab, 1, half * 2 + low), 2)
        return carry

    def load(h, ref):
        return pltpu.make_async_copy(ref, weights.at[pl.ds(h * VB, VB)], w_sems.at[h])

    @pl.when(step == 0)
    def _():
        issue(step, 0)
        for h, ref in enumerate((own_ref, other_ref)):
            load(h, ref).start()

    @pl.when(step < 3)
    def _():
        issue(step + 1, 0)

    @pl.when(step == 0)
    def _():
        for h, ref in enumerate((own_ref, other_ref)):
            load(h, ref).wait()

    pltpu.make_async_copy(xt.at[step], xt.at[step], sems.at[step]).wait()
    pltpu.make_async_copy(squares.at[step], squares.at[step], sems.at[step]).wait()
    pltpu.make_async_copy(xt.at[step], xt_out.at[step], out_sems.at[step]).start()
    acc[...] = jnp.dot(weights[...], xt[step], preferred_element_type=F32)
    mean = jnp.sum(squares[step].astype(F32), axis=0, keepdims=True) / D
    rinv = lax.rsqrt(mean + EPS)
    z = at_of(tab, 2, step)
    rinv_ref[z] = rinv
    rows = 64

    def chunk(i, total):
        here = pl.ds(pl.multiple_of(i * rows, rows), rows)
        act = acc[here, :] * rinv
        act_ref[0, here, :] = act
        return total + jnp.exp(jnp.tanh(act * (1.0 / CAP)) * CAP)

    total = lax.fori_loop(0, 2 * VB // rows, chunk, jnp.zeros((rows, 2 * TB), F32))
    total = jnp.sum(total, axis=0, keepdims=True)
    for yhi in range(2):
        total_ref[pl.ds(z * 2 + yhi, 1), :] = total[:, yhi * TB : (yhi + 1) * TB]

    @pl.when(step == 3)
    def _():
        for tile in range(4):
            pltpu.make_async_copy(xt.at[tile], xt_out.at[tile], out_sems.at[tile]).wait()


ANYWHERE = pl.BlockSpec(memory_space=pl.ANY)
SMEM_SPEC = pl.BlockSpec(memory_space=pltpu.SMEM)
VMEM_SPEC = pl.BlockSpec(memory_space=pltpu.VMEM)


def act_call(tab, halves, own, other):
    return pl.pallas_call(
        act_kernel,
        grid_spec=pltpu.PrefetchScalarGridSpec(
            num_scalar_prefetch=1,
            grid=(4,),
            in_specs=[ANYWHERE] * 8,
            out_specs=[
                pl.BlockSpec((1, 2 * VB, 2 * TB), lambda z, w: (z, 0, 0)),
                pl.BlockSpec((8, TB), lambda z, w: (0, 0)),
                pl.BlockSpec((4, 1, 2 * TB), lambda z, w: (0, 0, 0)),
                ANYWHERE,
            ],
            scratch_shapes=[
                pltpu.VMEM((4, D, 2 * TB), BF),
                pltpu.VMEM((4, 8 * SQ, 2 * TB), BF),
                pltpu.VMEM((2 * VB, D), BF),
                pltpu.VMEM((2 * VB, 2 * TB), F32),
                pltpu.SemaphoreType.DMA((4,)),
                pltpu.SemaphoreType.DMA((4,)),
                pltpu.SemaphoreType.DMA((2,)),
            ],
        ),
        out_shape=[
            jax.ShapeDtypeStruct((4, 2 * VB, 2 * TB), F32),
            jax.ShapeDtypeStruct((8, TB), F32),
            jax.ShapeDtypeStruct((4, 1, 2 * TB), F32),
            jax.ShapeDtypeStruct((4, D, 2 * TB), BF),
        ],
        compiler_params=pltpu.CompilerParams(vmem_limit_bytes=VMEM),
        cost_estimate=pl.CostEstimate(
            flops=2 * 1024 * 1024 * D, bytes_accessed=30_000_000, transcendentals=2 << 20
        ),
        name="act",
    )(tab, *halves, own, other)


def prep_kernel(tab, act_ref, tgt_ref, expo_ref, stat_ref, bend_ref):
    step = pl.program_id(0)
    z = at_of(tab, 2, step)
    tgt = tgt_ref[z]
    rows = 32
    zeros = jnp.zeros((rows, 2 * TB), F32)
    sums = (zeros, zeros, zeros, zeros)
    for h in range(2):
        row0 = lax.broadcasted_iota(jnp.int32, (rows, 2 * TB), 0) + tab[24 + h]

        def chunk(i, sums, h=h, row0=row0):
            picked, slope, slope_at, bend = sums
            at = pl.multiple_of(i * rows, rows)
            here = pl.ds(h * VB + at, rows)
            act = act_ref[0, here, :]
            t = jnp.tanh(act * (1.0 / CAP))
            capped = t * CAP
            bent = 1.0 - t * t
            expo = jnp.exp(capped) * bent
            expo_ref[0, here, :] = expo
            hit = row0 + at == tgt
            return (
                picked + jnp.where(hit, capped, 0.0),
                slope + expo * act,
                slope_at + jnp.where(hit, bent * act, 0.0),
                bend + jnp.where(hit, bent, 0.0),
            )

        sums = lax.fori_loop(0, VB // rows, chunk, sums)
    sums = [jnp.sum(s, axis=0, keepdims=True) for s in sums]
    for i in range(3):
        for yhi in range(2):
            stat_ref[i, pl.ds(z * 2 + yhi, 1), :] = sums[i][:, yhi * TB : (yhi + 1) * TB]
    bend_ref[0] = sums[3]


def prep_call(tab, act, tgt):
    tile = pl.BlockSpec((1, 2 * VB, 2 * TB), lambda z, w: (z, 0, 0))
    return pl.pallas_call(
        prep_kernel,
        grid_spec=pltpu.PrefetchScalarGridSpec(
            num_scalar_prefetch=1,
            grid=(4,),
            in_specs=[tile, pl.BlockSpec((4, 1, 2 * TB), lambda z, w: (0, 0, 0))],
            out_specs=[
                tile,
                pl.BlockSpec((3, 8, TB), lambda z, w: (0, 0, 0)),
                pl.BlockSpec((1, 1, 2 * TB), lambda z, w: (z, 0, 0)),
            ],
        ),
        out_shape=[
            jax.ShapeDtypeStruct((4, 2 * VB, 2 * TB), F32),
            jax.ShapeDtypeStruct((3, 8, TB), F32),
            jax.ShapeDtypeStruct((4, 1, 2 * TB), F32),
        ],
        compiler_params=pltpu.CompilerParams(vmem_limit_bytes=VMEM),
        cost_estimate=pl.CostEstimate(
            flops=16 << 20, bytes_accessed=8 << 20, transcendentals=2 << 20
        ),
        name="prep",
    )(tab, act, tgt)


def pieces(tab, lead, gz, gy, w0, w1, w2, outs):
    out0, out1, out2 = outs
    for low in range(2):
        place = lead * 2 + low
        got = jnp.dot(
            w0[...].reshape(8 * PT, 2 * VB), gz[place], preferred_element_type=F32
        ).astype(BF)
        for x in range(4):
            for ylo in range(2):
                for yhi in range(2):
                    at = (low * 4 + place_of(tab, 1, yhi * 2 + ylo)) * 4 + place_of(tab, 0, x)
                    row = (x * 2 + ylo) * PT
                    out0[at] = got[row : row + PT, yhi * TB : (yhi + 1) * TB]
    for low in range(2):
        x = at_of(tab, 0, lead * 2 + low)
        w = w1[x].reshape(2 * PT, 2 * VB)
        for z in range(4):
            got = jnp.dot(w, gz[z], preferred_element_type=F32).astype(BF)
            for ylo in range(2):
                for yhi in range(2):
                    at = (low * 4 + z) * 4 + place_of(tab, 1, yhi * 2 + ylo)
                    out1[at] = got[ylo * PT : (ylo + 1) * PT, yhi * TB : (yhi + 1) * TB]
    for low in range(2):
        y = at_of(tab, 1, lead * 2 + low)
        w = w2[y & 1].reshape(4 * PT, 2 * VB)
        for pair in range(2):
            got = jnp.dot(w, gy[y >> 1, pair], preferred_element_type=F32).astype(BF)
            for x in range(4):
                for z in range(2):
                    at = (low * 4 + place_of(tab, 0, x)) * 4 + 2 * pair + z
                    out2[at] = got[x * PT : (x + 1) * PT, z * TB : (z + 1) * TB]


def grad_kernel(tab, expo_ref, bend_ref, totals_ref, rinv_ref, tgt_ref, w0, w1, w2, *outs):
    gz, gr, gy = outs[:3]
    rows = 32
    inv = 1.0 / jnp.sum(totals_ref[...], axis=0)
    line = lax.broadcasted_iota(jnp.int32, (8, TB), 0)

    def chunk(i, carry, place, h, inv_z, rinv, bend, tgt, row0):
        at = pl.multiple_of(i * rows, rows)
        here = pl.ds(h * VB + at, rows)
        g = expo_ref[place, here, :] * inv_z - jnp.where(row0 + at == tgt, bend, 0.0)
        gr[place, here, :] = (g * rinv).astype(BF)
        g = g.astype(BF)
        gz[place, here, :] = g
        for yhi in range(2):
            gy[yhi, place // 2, here, pl.ds(place % 2 * TB, TB)] = g[:, yhi * TB : (yhi + 1) * TB]
        return carry

    for place in range(4):
        z = at_of(tab, 2, place)
        inv_z = jnp.concatenate(
            [
                jnp.sum(jnp.where(line == z * 2 + yhi, inv, 0.0), axis=0, keepdims=True)
                for yhi in range(2)
            ],
            axis=1,
        )
        for h in range(2):
            row0 = lax.broadcasted_iota(jnp.int32, (rows, 2 * TB), 0) + tab[24 + h]
            lax.fori_loop(
                0,
                VB // rows,
                functools.partial(
                    chunk, place=place, h=h, inv_z=inv_z, rinv=rinv_ref[z],
                    bend=bend_ref[place], tgt=tgt_ref[z], row0=row0,
                ),
                0,
            )
    pieces(tab, 1, gz, gy, w0, w1, w2, outs[3:])


def keep_kernel(tab, gz, gy, w0, w1, w2, *outs):
    pieces(tab, 0, gz, gy, w0, w1, w2, outs)


HALF = jax.ShapeDtypeStruct((32, PT, TB), BF)


def grad_call(tab, expo, bend, totals, rinv, tgt, turned):
    shapes = [
        jax.ShapeDtypeStruct((4, 2 * VB, 2 * TB), BF),
        jax.ShapeDtypeStruct((4, 2 * VB, 2 * TB), BF),
        jax.ShapeDtypeStruct((2, 2, 2 * VB, 2 * TB), BF),
    ] + [HALF] * 3
    return pl.pallas_call(
        grad_kernel,
        in_specs=[SMEM_SPEC] + [VMEM_SPEC] * 8,
        out_specs=[VMEM_SPEC] * 6,
        out_shape=shapes,
        compiler_params=pltpu.CompilerParams(vmem_limit_bytes=VMEM),
        cost_estimate=pl.CostEstimate(
            flops=1024 * 1024 * D, bytes_accessed=24_000_000, transcendentals=0
        ),
        name="grad",
    )(tab, expo, bend, totals, rinv, tgt, *turned)


def keep_call(tab, gz, gy, turned):
    return pl.pallas_call(
        keep_kernel,
        in_specs=[SMEM_SPEC] + [VMEM_SPEC] * 5,
        out_specs=[VMEM_SPEC] * 3,
        out_shape=[HALF] * 3,
        compiler_params=pltpu.CompilerParams(vmem_limit_bytes=VMEM),
        cost_estimate=pl.CostEstimate(
            flops=1024 * 1024 * D, bytes_accessed=18_000_000, transcendentals=0
        ),
        name="keep",
    )(tab, gz, gy, *turned)


def head_kernel(gr, xt, own_w, other_w, own_ref, other_ref, gain_ref):
    gain = None
    for h, (w, ref) in enumerate(((own_w, own_ref), (other_w, other_ref))):
        total = None
        for z in range(4):
            part = lax.dot_general(
                gr[z, h * VB : (h + 1) * VB, :], xt[z],
                (((1,), (1,)), ((), ())), preferred_element_type=F32,
            )
            total = part if total is None else total + part
        ref[...] = total.astype(BF)
        here = jnp.sum(total * w[...].astype(F32), axis=0, keepdims=True)
        gain = here if gain is None else gain + here
    gain_ref[...] = gain


def head_call(gr, xt, own, other, half):
    tile = 768
    tiles = D // 2 // tile
    cols = pl.BlockSpec((VB, tile), lambda f: (0, f + half * tiles))
    return pl.pallas_call(
        head_kernel,
        grid=(tiles,),
        in_specs=[
            pl.BlockSpec((4, 2 * VB, 2 * TB), lambda f: (0, 0, 0), pipeline_mode=pl.Buffered(1)),
            pl.BlockSpec((4, tile, 2 * TB), lambda f: (0, f + half * tiles, 0)),
            cols,
            cols,
        ],
        out_specs=[pl.BlockSpec((VB, tile), lambda f: (0, f))] * 2
        + [pl.BlockSpec((1, tile), lambda f: (0, f))],
        out_shape=[jax.ShapeDtypeStruct((VB, D // 2), BF)] * 2
        + [jax.ShapeDtypeStruct((1, D // 2), F32)],
        compiler_params=pltpu.CompilerParams(vmem_limit_bytes=VMEM),
        cost_estimate=pl.CostEstimate(
            flops=1024 * 1024 * D, bytes_accessed=16_000_000, transcendentals=0
        ),
        name="head",
    )(gr, xt, own, other)


def shards(section_output, norm_gain, head_weight, targets):
    x, ylo, yhi, z, core = (lax.axis_index(a) for a in AX)
    y = yhi * 2 + ylo
    shard = (((x * 2 + ylo) * 2 + yhi) * 4 + z) * 2 + core
    tab = table(x, y, z, core, shard)

    xt = section_output.T.astype(F32)
    gain = norm_gain.astype(F32)[:, None]
    scaled_x = (xt * gain).astype(BF)
    squares = jnp.sum(xt * xt, axis=0, keepdims=True)
    extra = jnp.concatenate(
        split3(squares) + [jnp.zeros((SQ - 3, TB), BF)], axis=0
    )
    blocks = [
        jnp.concatenate([scaled_x[:PT], extra], axis=0),
        scaled_x[PT : 2 * PT],
        scaled_x[2 * PT :],
    ]
    other = send(head_weight, TWIN)
    turned = flip(head_weight, other)

    tgt = lax.dynamic_index_in_dim(
        targets.reshape(2, 4, 2, TB), core, axis=2, keepdims=False
    ).transpose(1, 0, 2).reshape(4, 1, 2 * TB)
    halves = gather(blocks)
    halves, turned, tgt, tab = lax.optimization_barrier((halves, turned, tgt, tab))

    act, total, rinv, xt_all = act_call(tab, halves, head_weight, other)
    totals = lax.all_to_all(
        jnp.broadcast_to(total[None], (64, 8, TB)), AX[:4], 0, 0
    )
    expo, stats, bend = prep_call(tab, act, tgt)

    out = grad_call(tab, expo, bend, totals, rinv, tgt, turned)
    gz, gr, gy = out[:3]
    kept = keep_call(tab, gz, gy, turned)
    own0, other0, gain0 = head_call(gr, xt_all, head_weight, other, 0)
    own1, other1, gain1 = head_call(gr, xt_all, head_weight, other, 1)
    sums = reduce_scatter(list(out[3:]), kept)
    head_grad = jnp.concatenate(
        [add(own0, send(other0, TWIN)), add(own1, send(other1, TWIN))], axis=1
    )

    by_owner = jnp.broadcast_to(
        stats.reshape(1, 1, 3, 4, 2, TB).transpose(0, 1, 4, 3, 2, 5).reshape(1, 2, 4, 3 * TB),
        (8, 2, 4, 3 * TB),
    )
    gains = jnp.concatenate([gain0, gain1], axis=1).reshape(8, 1, 1, FB)
    gains = jnp.concatenate([gains, jnp.zeros((8, 1, 1, TB // 2), F32)], axis=3)
    mixed = jnp.concatenate(
        [by_owner, jnp.broadcast_to(gains, (8, 2, 4, 5 * TB))], axis=3
    ).reshape(64, 8, TB)
    mixed = jnp.sum(lax.all_to_all(mixed, AX[:4], 0, 0), axis=0)
    picked, slope, slope_at = mixed[0:1], mixed[1:2], mixed[2:3]
    gain_part = mixed[3:].reshape(5 * TB)[:FB]
    gain_grad = (gain_part + send(gain_part, TWIN)) / norm_gain.astype(F32)

    row = jnp.sum(totals, axis=0)
    total = lax.dynamic_slice(row, (z * 2 + yhi, 0), (1, TB))
    rinv = lax.dynamic_slice(rinv, (z, 0, yhi * TB), (1, 1, TB)).reshape(1, TB)
    token_loss = (jnp.log(total) - picked).reshape(TB)
    inner = slope / total - slope_at
    grad_hidden = jnp.concatenate(sums, axis=0)
    grad_input = (rinv * (grad_hidden * gain) - xt * (rinv * rinv * inner / D)).astype(BF).T
    return (token_loss, grad_input, head_grad, gain_grad)


def solution(mesh):
    fine = Mesh(mesh.devices.reshape(4, 2, 2, 4, 2), AX)
    pipe, dp = ("x", "ylo"), ("yhi", "z", "core")
    return jax.shard_map(
        shards,
        mesh=fine,
        in_specs=(P(dp, pipe), P(pipe), P(pipe + dp, None), P()),
        out_specs=(P(dp), P(dp, pipe), P(pipe + dp, None), P(pipe)),
        check_vma=False,
    )
```

```python
import functools
import itertools

import jax
import jax.numpy as jnp
import numpy as np
from jax import lax
from jax.experimental import pallas as pl
from jax.experimental.pallas import tpu as pltpu
from jax.sharding import Mesh, PartitionSpec as P

AX = ("x", "ylo", "yhi", "z", "core")
D = 4608
FB = 576
PT = 192
SQ = 16
TB = 128
VB = 512
CAP = 30.0
EPS = 1e-06
VMEM = 60 * 1024 * 1024
BF = jnp.bfloat16
F32 = jnp.float32

ORDER = ((0, 1, 2), (1, 2, 0), (2, 0, 1))


def coords(i):
    core, z, yhi, ylo, x = i % 2, i // 2 % 4, i // 8 % 2, i // 16 % 2, i // 32
    return [x, yhi * 2 + ylo, z], core


def number(c, core):
    return (((c[0] * 2 + c[1] % 2) * 2 + c[1] // 2) * 4 + c[2]) * 2 + core


def from_bits(core, late, early):
    gray = late * 2 + early if core == 0 else early * 2 + late
    return gray ^ (gray >> 1)


BITS = list(itertools.product((0, 1), repeat=3))
CUBES = [
    [number([from_bits(core, b, e) for b, e in zip(late, early)], core) for early in BITS]
    for core in (0, 1)
    for late in BITS
]
TWIN = [(i, i ^ 1) for i in range(128)]


@functools.cache
def across(dim):
    pairs = []
    for i in range(128):
        c, core = coords(i)
        gray = (c[dim] ^ (c[dim] >> 1)) ^ (2 if core == 0 else 1)
        c[dim] = gray ^ (gray >> 1)
        pairs.append((i, number(c, core)))
    return pairs


def send(a, pairs):
    return lax.ppermute(a, AX, pairs)


def in_cube(a):
    return lax.all_to_all(a, AX, 0, 0, axis_index_groups=CUBES)


def gather(block):
    cube = in_cube(jnp.broadcast_to(block[None], (8,) + block.shape))
    cuts = (0, PT + SQ, 2 * PT + SQ, 3 * PT + SQ)
    held = [cube[:, cuts[p] : cuts[p + 1]] for p in range(3)]
    for phase in range(2):
        got = [send(held[p], across(ORDER[p][phase])) for p in range(3)]
        held = [jnp.concatenate([held[p], got[p]]) for p in range(3)]
    got = [send(held[p], across(ORDER[p][2])) for p in range(3)]
    return [a for p in range(3) for a in (held[p], got[p])]


def block_at(part, places):
    late = [place >> 1 for place in places]
    early = [place & 1 for place in places]
    first, second, _ = ORDER[part]
    return (late[second] * 2 + late[first]) * 8 + early[0] * 4 + early[1] * 2 + early[2]


def total(arrays):
    return functools.reduce(lambda a, b: a + b, [a.astype(F32) for a in arrays])


def split3(v):
    hi = lax.reduce_precision(v, 8, 7)
    mid = lax.reduce_precision(v - hi, 8, 7)
    lo = v - hi - mid
    return [hi.astype(BF), mid.astype(BF), lo.astype(BF)]


def add(a, b):
    return (a.astype(F32) + b.astype(F32)).astype(a.dtype)


def table(x, y, z, core, shard):
    out = []
    place = jnp.arange(4, dtype=jnp.int32)

    def swap(bits):
        return jnp.where(core == 0, bits, (bits & 1) * 2 + (bits >> 1))

    mine = [swap(c ^ (c >> 1)) & 2 for c in (x, y, z)]
    for late in mine:
        gray = swap(place ^ late)
        out.append(gray ^ (gray >> 1))
    for late in mine:
        out.append(swap(place ^ (place >> 1)) ^ late)
    out.append(jnp.stack([shard * VB, (shard ^ 1) * VB]))
    return jnp.concatenate(out).astype(jnp.int32)


def at_of(tab, dim, place):
    return tab[4 * dim + place]


def place_of(tab, dim, at):
    return tab[12 + 4 * dim + at]


def flip_kernel(own_ref, other_ref, a_ref, b_ref, c_ref):
    for h, ref in enumerate((own_ref, other_ref)):
        turned = ref[...].T
        cols = pl.ds(h * VB, VB)
        for ylo in range(2):
            at = ylo * FB
            a_ref[0, ylo, :, cols] = turned[at : at + PT]
            b_ref[0, ylo, :, cols] = turned[at + PT : at + 2 * PT]
            c_ref[ylo, 0, :, cols] = turned[at + 2 * PT : at + 3 * PT]


def flip(own, other):
    block = pl.BlockSpec((VB, 2 * FB), lambda x: (0, x))
    return pl.pallas_call(
        flip_kernel,
        grid=(4,),
        in_specs=[block, block],
        out_specs=[
            pl.BlockSpec((1, 2, PT, 2 * VB), lambda x: (x, 0, 0, 0)),
            pl.BlockSpec((1, 2, PT, 2 * VB), lambda x: (x, 0, 0, 0)),
            pl.BlockSpec((2, 1, PT, 2 * VB), lambda x: (0, x, 0, 0)),
        ],
        out_shape=[
            jax.ShapeDtypeStruct((4, 2, PT, 2 * VB), BF),
            jax.ShapeDtypeStruct((4, 2, PT, 2 * VB), BF),
            jax.ShapeDtypeStruct((2, 4, PT, 2 * VB), BF),
        ],
        compiler_params=pltpu.CompilerParams(vmem_limit_bytes=VMEM),
        cost_estimate=pl.CostEstimate(
            flops=0, bytes_accessed=4 * VB * D * 2, transcendentals=0
        ),
        name="flip",
    )(own, other)


def act_kernel(tab, *refs):
    halves = [refs[2 * p : 2 * p + 2] for p in range(3)]
    own_ref, other_ref, tgt_ref = refs[6:9]
    expo_ref, bend_ref, rinv_ref, stat_ref, xt_out = refs[9:14]
    xt, squares, weights, acc, totals, stats, sems, out_sems, w_sems = refs[14:]
    step = pl.program_id(0)

    def fetch(src, tile, x, y, part):
        row = (x * 2 + (y & 1)) * FB + part * PT
        lanes = pl.ds(pl.multiple_of((y >> 1) * TB, TB), TB)
        pltpu.make_async_copy(
            src.at[pl.ds(0, PT)],
            xt.at[tile, pl.ds(pl.multiple_of(row, 16), PT), lanes],
            sems.at[tile],
        ).start()
        if part == 0:
            row = (x * 2 + (y & 1)) * SQ
            pltpu.make_async_copy(
                src.at[pl.ds(PT, SQ)],
                squares.at[tile, pl.ds(pl.multiple_of(row, 16), SQ), lanes],
                sems.at[tile],
            ).start()

    def issue(tile):
        for px in range(4):
            for py in range(4):
                x, y = at_of(tab, 0, px), at_of(tab, 1, py)
                places = (px, py, tile)
                fetch(halves[1][px >> 1].at[block_at(1, places)], tile, x, y, 1)
                fetch(halves[2][py >> 1].at[block_at(2, places)], tile, x, y, 2)
        for half in range(2):
            @pl.when((tile >> 1) == half)
            def _():
                for px in range(4):
                    for py in range(4):
                        fetch(
                            halves[0][half].at[block_at(0, (px, py, tile))],
                            tile, at_of(tab, 0, px), at_of(tab, 1, py), 0,
                        )

    def load(h, ref):
        return pltpu.make_async_copy(ref, weights.at[pl.ds(h * VB, VB)], w_sems.at[h])

    def arrived():
        pltpu.make_async_copy(xt.at[step], xt.at[step], sems.at[step]).wait()
        pltpu.make_async_copy(squares.at[step], squares.at[step], sems.at[step]).wait()
        pltpu.make_async_copy(xt.at[step], xt_out.at[step], out_sems.at[step]).start()

    @pl.when(step == 0)
    def _():
        issue(step)
        for h, ref in enumerate((own_ref, other_ref)):
            load(h, ref).start()
        issue(step + 1)
        arrived()
        for h, ref in enumerate((own_ref, other_ref)):
            load(h, ref).wait()
            rows = pl.ds(h * VB, VB)
            acc[rows, :] = jnp.dot(weights[rows, :], xt[step], preferred_element_type=F32)

    @pl.when(step > 0)
    def _():
        @pl.when(step < 3)
        def _():
            issue(step + 1)

        arrived()
        acc[...] = jnp.dot(weights[...], xt[step], preferred_element_type=F32)

    mean = jnp.sum(squares[step].astype(F32), axis=0, keepdims=True) / D
    rinv = lax.rsqrt(mean + EPS)
    z = at_of(tab, 2, step)
    rinv_ref[z] = rinv
    tgt = tgt_ref[z]
    rows = 32
    zeros = jnp.zeros((8, 2 * TB), F32)
    sums = (zeros,) * 3
    inside = jnp.zeros((1, 2 * TB), jnp.bool_)

    def fold(v):
        return jnp.sum(v.reshape(rows // 8, 8, 2 * TB), axis=0)

    for h in range(2):
        row0 = lax.broadcasted_iota(jnp.int32, (rows, 2 * TB), 0) + tab[24 + h]
        inside = inside | ((tgt >= tab[24 + h]) & (tgt < tab[24 + h] + VB))

        def chunk(i, sums, h=h, row0=row0):
            total, slope, act_at = sums
            at = pl.multiple_of(i * rows, rows)
            here = pl.ds(h * VB + at, rows)
            act = acc[here, :] * rinv
            t = jnp.tanh(act * (1.0 / CAP))
            expo = jnp.exp(t * CAP)
            sharp = expo * (1.0 - t * t)
            expo_ref[0, here, :] = sharp
            return (
                total + fold(expo),
                slope + fold(sharp * act),
                act_at + fold(jnp.where(row0 + at == tgt, act, 0.0)),
            )

        sums = lax.fori_loop(0, VB // rows, chunk, sums)
    total, slope, act_at = [jnp.sum(s, axis=0, keepdims=True) for s in sums]
    t = jnp.tanh(act_at * (1.0 / CAP))
    bend = jnp.where(inside, 1.0 - t * t, 0.0)
    bend_ref[0] = bend
    sums = (total, t * CAP, slope, bend * act_at)
    for yhi in range(2):
        lanes = slice(yhi * TB, (yhi + 1) * TB)
        totals[pl.ds(z * 2 + yhi, 1), :] = sums[0][:, lanes]
        stats[yhi * 4 + z] = jnp.concatenate(
            [s[:, lanes] for s in sums[1:4]] + [jnp.zeros((5, TB), F32)], axis=0
        )

    @pl.when(step == 3)
    def _():
        for chip in range(64):
            stat_ref[chip, 0:8, :] = totals[...]
            stat_ref[chip, 8:16, :] = stats[chip % 8]
        for tile in range(4):
            pltpu.make_async_copy(xt.at[tile], xt_out.at[tile], out_sems.at[tile]).wait()


ANYWHERE = pl.BlockSpec(memory_space=pl.ANY)
SMEM_SPEC = pl.BlockSpec(memory_space=pltpu.SMEM)
VMEM_SPEC = pl.BlockSpec(memory_space=pltpu.VMEM)


def act_call(tab, halves, own, other, tgt):
    tile = pl.BlockSpec((1, 2 * VB, 2 * TB), lambda z, w: (z, 0, 0))
    rows = pl.BlockSpec((4, 1, 2 * TB), lambda z, w: (0, 0, 0))
    return pl.pallas_call(
        act_kernel,
        grid_spec=pltpu.PrefetchScalarGridSpec(
            num_scalar_prefetch=1,
            grid=(4,),
            in_specs=[ANYWHERE] * 8 + [rows],
            out_specs=[
                tile,
                pl.BlockSpec((1, 1, 2 * TB), lambda z, w: (z, 0, 0)),
                rows,
                pl.BlockSpec((64, 16, TB), lambda z, w: (0, 0, 0)),
                ANYWHERE,
            ],
            scratch_shapes=[
                pltpu.VMEM((4, D, 2 * TB), BF),
                pltpu.VMEM((4, 8 * SQ, 2 * TB), BF),
                pltpu.VMEM((2 * VB, D), BF),
                pltpu.VMEM((2 * VB, 2 * TB), F32),
                pltpu.VMEM((8, TB), F32),
                pltpu.VMEM((8, 8, TB), F32),
                pltpu.SemaphoreType.DMA((4,)),
                pltpu.SemaphoreType.DMA((4,)),
                pltpu.SemaphoreType.DMA((2,)),
            ],
        ),
        out_shape=[
            jax.ShapeDtypeStruct((4, 2 * VB, 2 * TB), F32),
            jax.ShapeDtypeStruct((4, 1, 2 * TB), F32),
            jax.ShapeDtypeStruct((4, 1, 2 * TB), F32),
            jax.ShapeDtypeStruct((64, 16, TB), F32),
            jax.ShapeDtypeStruct((4, D, 2 * TB), BF),
        ],
        compiler_params=pltpu.CompilerParams(vmem_limit_bytes=VMEM),
        cost_estimate=pl.CostEstimate(
            flops=2 * 1024 * 1024 * D, bytes_accessed=30_000_000, transcendentals=2 << 20
        ),
        name="act",
    )(tab, *halves, own, other, tgt)


def pieces(tab, lead, gz, gy, weights, outs, ready, done):
    w0, w1, w2 = weights
    out0, out1, out2 = outs
    ready(0)
    w = w0[...].reshape(8 * PT, 2 * VB)
    both = jnp.concatenate([gz[lead * 2], gz[lead * 2 + 1]], axis=1)
    got = jnp.dot(w, both, preferred_element_type=F32).astype(BF)
    for low in range(2):
        for x in range(4):
            for ylo in range(2):
                for yhi in range(2):
                    places = (place_of(tab, 0, x), place_of(tab, 1, yhi * 2 + ylo), lead * 2 + low)
                    row, lane = (x * 2 + ylo) * PT, (low * 2 + yhi) * TB
                    out0[block_at(0, places)] = got[row : row + PT, lane : lane + TB]
    done(0)
    ready(1)
    for low in range(2):
        place = lead * 2 + low
        x = at_of(tab, 0, place)
        w = w1[x].reshape(2 * PT, 2 * VB)
        tokens = jnp.concatenate([gz[z] for z in range(4)], axis=1)
        got = jnp.dot(w, tokens, preferred_element_type=F32).astype(BF)
        for z in range(4):
            for ylo in range(2):
                for yhi in range(2):
                    places = (place, place_of(tab, 1, yhi * 2 + ylo), z)
                    row, lane = ylo * PT, (z * 2 + yhi) * TB
                    out1[block_at(1, places)] = got[row : row + PT, lane : lane + TB]
    done(1)
    ready(2)
    for low in range(2):
        place = lead * 2 + low
        y = at_of(tab, 1, place)
        w = w2[y & 1].reshape(4 * PT, 2 * VB)
        tokens = jnp.concatenate([gy[y >> 1, pair] for pair in range(2)], axis=1)
        got = jnp.dot(w, tokens, preferred_element_type=F32).astype(BF)
        for x in range(4):
            for z in range(4):
                places = (place_of(tab, 0, x), place, z)
                out2[block_at(2, places)] = got[x * PT : (x + 1) * PT, z * TB : (z + 1) * TB]
    done(2)


def copies(pairs, sems):
    return [
        pltpu.make_async_copy(src, dst, sems.at[i]) for i, (src, dst) in enumerate(pairs)
    ]


def grad_kernel(tab, expo_ref, bend_ref, totals_ref, rinv_ref, tgt_ref, *refs):
    w_refs, out_refs = refs[:3], refs[3:9]
    expo, w0, w1, w2, gz, gr, gy, away0, away1, away2, in_sems, out_sems = refs[9:]
    weights, away = (w0, w1, w2), (away0, away1, away2)
    tiles = [(expo_ref.at[i], expo.at[i]) for i in range(4)]
    incoming = copies(tiles + list(zip(w_refs, weights)), in_sems)
    outgoing = copies(list(zip((gz, gr, gy) + away, out_refs)), out_sems)
    for copy in incoming:
        copy.start()
    rows = 32
    inv = 1.0 / jnp.sum(totals_ref[...], axis=0)[0:8]
    line = lax.broadcasted_iota(jnp.int32, (8, TB), 0)

    def chunk(i, carry, place, h, inv_z, rinv, bend, tgt, row0):
        at = pl.multiple_of(i * rows, rows)
        here = pl.ds(h * VB + at, rows)
        g = expo[place, here, :] * inv_z - jnp.where(row0 + at == tgt, bend, 0.0)
        gr[place, here, :] = (g * rinv).astype(BF)
        g = g.astype(BF)
        gz[place, here, :] = g
        for yhi in range(2):
            gy[yhi, place // 2, here, pl.ds(place % 2 * TB, TB)] = g[:, yhi * TB : (yhi + 1) * TB]
        return carry

    for place in range(4):
        z = at_of(tab, 2, place)
        inv_z = jnp.concatenate(
            [
                jnp.sum(jnp.where(line == z * 2 + yhi, inv, 0.0), axis=0, keepdims=True)
                for yhi in range(2)
            ],
            axis=1,
        )
        incoming[place].wait()
        for h in range(2):
            row0 = lax.broadcasted_iota(jnp.int32, (rows, 2 * TB), 0) + tab[24 + h]
            lax.fori_loop(
                0,
                VB // rows,
                functools.partial(
                    chunk, place=place, h=h, inv_z=inv_z, rinv=rinv_ref[z],
                    bend=bend_ref[place], tgt=tgt_ref[z], row0=row0,
                ),
                0,
            )
    for copy in outgoing[:3]:
        copy.start()
    pieces(
        tab, 1, gz, gy, weights, away,
        lambda p: incoming[4 + p].wait(), lambda p: outgoing[3 + p].start(),
    )
    for copy in outgoing:
        copy.wait()


def keep_kernel(tab, gz_ref, gy_ref, *refs):
    w_refs, out_refs = refs[:3], refs[3:6]
    gz, w0, w1, gy, w2, kept0, kept1, kept2, in_sems, out_sems = refs[6:]
    kept = (kept0, kept1, kept2)
    incoming = copies(
        [(gz_ref, gz), (w_refs[0], w0), (w_refs[1], w1), (gy_ref, gy), (w_refs[2], w2)], in_sems
    )
    outgoing = copies(list(zip(kept, out_refs)), out_sems)
    for copy in incoming:
        copy.start()

    def ready(p):
        for copy in ((0, 1), (2,), (3, 4))[p]:
            incoming[copy].wait()

    pieces(tab, 0, gz, gy, (w0, w1, w2), kept, ready, lambda p: outgoing[p].start())
    for copy in outgoing:
        copy.wait()


HALF = (32, PT, TB)
GZ = (4, 2 * VB, 2 * TB)
GY = (2, 2, 2 * VB, 2 * TB)
W_SHAPES = ((4, 2, PT, 2 * VB), (4, 2, PT, 2 * VB), (2, 4, PT, 2 * VB))


def bf16_out(*shapes):
    return [jax.ShapeDtypeStruct(shape, BF) for shape in shapes]


def bf16_vmem(*shapes):
    return [pltpu.VMEM(shape, BF) for shape in shapes]


def grad_call(tab, expo, bend, totals, rinv, tgt, turned):
    return pl.pallas_call(
        grad_kernel,
        in_specs=[SMEM_SPEC, ANYWHERE] + [VMEM_SPEC] * 4 + [ANYWHERE] * 3,
        out_specs=[ANYWHERE] * 6,
        out_shape=bf16_out(GZ, GZ, GY, HALF, HALF, HALF),
        scratch_shapes=[pltpu.VMEM(GZ, F32)]
        + bf16_vmem(*W_SHAPES, GZ, GZ, GY, HALF, HALF, HALF)
        + [pltpu.SemaphoreType.DMA((7,)), pltpu.SemaphoreType.DMA((6,))],
        compiler_params=pltpu.CompilerParams(vmem_limit_bytes=VMEM),
        cost_estimate=pl.CostEstimate(
            flops=1024 * 1024 * D, bytes_accessed=24_000_000, transcendentals=0
        ),
        name="grad",
    )(tab, expo, bend, totals, rinv, tgt, *turned)


def keep_call(tab, gz, gy, turned):
    return pl.pallas_call(
        keep_kernel,
        in_specs=[SMEM_SPEC] + [ANYWHERE] * 5,
        out_specs=[ANYWHERE] * 3,
        out_shape=bf16_out(HALF, HALF, HALF),
        scratch_shapes=bf16_vmem(
            GZ, W_SHAPES[0], W_SHAPES[1], GY, W_SHAPES[2], HALF, HALF, HALF
        )
        + [pltpu.SemaphoreType.DMA((5,)), pltpu.SemaphoreType.DMA((3,))],
        compiler_params=pltpu.CompilerParams(vmem_limit_bytes=VMEM),
        cost_estimate=pl.CostEstimate(
            flops=1024 * D, bytes_accessed=1_000_000, transcendentals=0
        ),
        name="keep",
    )(tab, gz, gy, *turned)


def head_kernel(gr, xt, own_w, other_w, own_ref, other_ref, gain_ref):
    got = lax.dot_general(
        jnp.concatenate([gr[z] for z in range(4)], axis=1),
        jnp.concatenate([xt[z] for z in range(4)], axis=1),
        (((1,), (1,)), ((), ())), preferred_element_type=F32,
    )
    own_ref[...] = got[:VB].astype(BF)
    other_ref[...] = got[VB:].astype(BF)
    gain_ref[...] = jnp.sum(
        got[:VB] * own_w[...].astype(F32) + got[VB:] * other_w[...].astype(F32),
        axis=0, keepdims=True,
    )


def head_call(gr, xt, own, other):
    tile = 768
    cols = pl.BlockSpec((VB, tile), lambda f: (0, f))
    return pl.pallas_call(
        head_kernel,
        grid=(D // tile,),
        in_specs=[
            pl.BlockSpec((4, 2 * VB, 2 * TB), lambda f: (0, 0, 0), pipeline_mode=pl.Buffered(1)),
            pl.BlockSpec((4, tile, 2 * TB), lambda f: (0, f, 0)),
            cols,
            cols,
        ],
        out_specs=[cols, cols, pl.BlockSpec((1, tile), lambda f: (0, f))],
        out_shape=bf16_out((VB, D), (VB, D)) + [jax.ShapeDtypeStruct((1, D), F32)],
        compiler_params=pltpu.CompilerParams(vmem_limit_bytes=VMEM),
        cost_estimate=pl.CostEstimate(
            flops=1024 * D, bytes_accessed=1_000_000, transcendentals=0
        ),
        name="head",
    )(gr, xt, own, other)


def last_kernel(*refs):
    out_ref = refs[-1]
    gain_ref = refs[-2]
    for p in range(3):
        here = refs[4 * p : 4 * p + 4]
        out_ref[:, p * PT : (p + 1) * PT, :] = total([a[...] for a in here]).astype(BF)
    out_ref[:, FB : FB + SQ, :] = gain_ref[...]


def last_call(here, gains):
    count = 2
    block = pl.BlockSpec((count, PT, TB), lambda i: (i, 0, 0))
    return pl.pallas_call(
        last_kernel,
        grid=(8 // count,),
        in_specs=[block] * 12 + [pl.BlockSpec((count, SQ, TB), lambda i: (i, 0, 0))],
        out_specs=pl.BlockSpec((count, FB + SQ, TB), lambda i: (i, 0, 0)),
        out_shape=jax.ShapeDtypeStruct((8, FB + SQ, TB), BF),
        compiler_params=pltpu.CompilerParams(vmem_limit_bytes=VMEM),
        cost_estimate=pl.CostEstimate(flops=4 << 20, bytes_accessed=6_000_000, transcendentals=0),
        name="last",
    )(*[a for part in here for a in part], gains)


def shards(section_output, norm_gain, head_weight, targets):
    x, ylo, yhi, z, core = (lax.axis_index(a) for a in AX)
    y = yhi * 2 + ylo
    shard = (((x * 2 + ylo) * 2 + yhi) * 4 + z) * 2 + core
    tab = table(x, y, z, core, shard)

    xt = section_output.T.astype(F32)
    gain = norm_gain.astype(F32)[:, None]
    scaled_x = (xt * gain).astype(BF)
    squares = jnp.sum(xt * xt, axis=0, keepdims=True)
    extra = jnp.concatenate(
        split3(squares) + [jnp.zeros((SQ - 3, TB), BF)], axis=0
    )
    block = jnp.concatenate([scaled_x[:PT], extra, scaled_x[PT:]], axis=0)
    other = send(head_weight, TWIN)
    turned = flip(head_weight, other)

    tgt = lax.dynamic_index_in_dim(
        targets.reshape(2, 4, 2, TB), core, axis=2, keepdims=False
    ).transpose(1, 0, 2).reshape(4, 1, 2 * TB)
    halves = gather(block)
    halves, turned, tgt, tab = lax.optimization_barrier((halves, turned, tgt, tab))

    expo, bend, rinv, stats, xt_all = act_call(tab, halves, head_weight, other, tgt)
    stats = lax.all_to_all(stats, AX[:4], 0, 0)

    gz, gr, gy, *away = grad_call(tab, expo, bend, stats, rinv, tgt, turned)

    bound = lax.optimization_barrier
    got = [send(away[p], across(ORDER[p][2])) for p in range(3)]
    own_part, other_part, gains = head_call(gr, xt_all, head_weight, other)
    gains, gz, gy = bound((gains, gz, gy))
    kept = keep_call(tab, gz, gy, turned)
    gains = gains.reshape(D // TB, TB)
    gains = gains + send(gains, TWIN)
    gains = gains + send(gains, across(2))
    got, kept, gains, own_part, other_part = bound((got, kept, gains, own_part, other_part))
    here = [[kept[p], got[p]] for p in range(3)]
    for phase, half in ((1, 16), (0, 8)):
        away = [total([a[half:2 * half] for a in here[p]]).astype(BF) for p in range(3)]
        away, gains, other_part = bound((away, gains, other_part))
        got = [send(away[p], across(ORDER[p][phase])) for p in range(3)]
        more = send(gains, across(phase))
        if phase == 1:
            other_part = send(other_part, TWIN)
        got, more, other_part = bound((got, more, other_part))
        gains = gains + more
        here = [here[p] + [got[p]] for p in range(3)]

    owner = jnp.stack([tab[ex] * 2 + (tab[4 + ey] & 1) for ex, ey, _ in BITS])
    chosen = owner[:, None, None] == jnp.arange(8, dtype=jnp.int32)[None, :, None]
    gains = jnp.sum(jnp.where(chosen, gains.reshape(1, 8, FB), 0.0), axis=1)
    gains = jnp.concatenate([gains, jnp.zeros((8, 5 * TB - FB), F32)], axis=1)
    gains = jnp.stack(split3(gains) + [jnp.zeros((8, 5 * TB), BF)], axis=1)
    gains = gains.reshape(8, 20, TB)[:, :SQ]

    blocks, own_part, other_part = bound((last_call(here, gains), own_part, other_part))
    blocks, head_grad = bound((in_cube(blocks), add(own_part, other_part)))
    blocks = jnp.sum(blocks.astype(F32), axis=0)
    grad_hidden = blocks[:FB]
    gains = jnp.sum(blocks[FB : FB + 15].reshape(3, 5 * TB), axis=0)[:FB]
    gain_grad = gains / norm_gain.astype(F32)

    row = jnp.sum(stats, axis=0)
    picked, slope, slope_at = row[8:9], row[9:10], row[10:11]
    sum_exp = lax.dynamic_slice(row, (z * 2 + yhi, 0), (1, TB))
    rinv = lax.dynamic_slice(rinv, (z, 0, yhi * TB), (1, 1, TB)).reshape(1, TB)
    token_loss = (jnp.log(sum_exp) - picked).reshape(TB)
    inner = slope / sum_exp - slope_at
    grad_input = (rinv * (grad_hidden * gain) - xt * (rinv * rinv * inner / D)).astype(BF).T
    return (token_loss, grad_input, head_grad, gain_grad)


def solution(mesh):
    fine = Mesh(mesh.devices.reshape(4, 2, 2, 4, 2), AX)
    pipe, dp = ("x", "ylo"), ("yhi", "z", "core")
    return jax.shard_map(
        shards,
        mesh=fine,
        in_specs=(P(dp, pipe), P(pipe), P(pipe + dp, None), P()),
        out_specs=(P(dp), P(dp, pipe), P(pipe + dp, None), P(pipe)),
        check_vma=False,
    )
```

```python
import functools
import itertools

import jax
import jax.numpy as jnp
import numpy as np
from jax import lax
from jax.experimental import pallas as pl
from jax.experimental.pallas import tpu as pltpu
from jax.sharding import Mesh, PartitionSpec as P

AX = ("x", "ylo", "yhi", "z", "core")
D = 4608
FB = 576
PT = 192
SQ = 16
TB = 128
VB = 512
CAP = 30.0
EPS = 1e-06
VMEM = 60 * 1024 * 1024
BF = jnp.bfloat16
F32 = jnp.float32

ORDER = ((0, 1, 2), (1, 2, 0), (2, 0, 1))


def coords(i):
    core, z, yhi, ylo, x = i % 2, i // 2 % 4, i // 8 % 2, i // 16 % 2, i // 32
    return [x, yhi * 2 + ylo, z], core


def number(c, core):
    return (((c[0] * 2 + c[1] % 2) * 2 + c[1] // 2) * 4 + c[2]) * 2 + core


def from_bits(core, late, early):
    gray = late * 2 + early if core == 0 else early * 2 + late
    return gray ^ (gray >> 1)


BITS = list(itertools.product((0, 1), repeat=3))
CUBES = [
    [number([from_bits(core, b, e) for b, e in zip(late, early)], core) for early in BITS]
    for core in (0, 1)
    for late in BITS
]
TWIN = [(i, i ^ 1) for i in range(128)]


@functools.cache
def across(dim):
    pairs = []
    for i in range(128):
        c, core = coords(i)
        gray = (c[dim] ^ (c[dim] >> 1)) ^ (2 if core == 0 else 1)
        c[dim] = gray ^ (gray >> 1)
        pairs.append((i, number(c, core)))
    return pairs


def send(a, pairs):
    return lax.ppermute(a, AX, pairs)


def in_cube(a):
    return lax.all_to_all(a, AX, 0, 0, axis_index_groups=CUBES)


def gather(block):
    cube = in_cube(jnp.broadcast_to(block[None], (8,) + block.shape))
    cuts = (0, PT + SQ, 2 * PT + SQ, 3 * PT + SQ)
    held = [cube[:, cuts[p] : cuts[p + 1]] for p in range(3)]
    for phase in range(2):
        got = [send(held[p], across(ORDER[p][phase])) for p in range(3)]
        held = [jnp.concatenate([held[p], got[p]]) for p in range(3)]
    got = [send(held[p], across(ORDER[p][2])) for p in range(3)]
    return [a for p in range(3) for a in (held[p], got[p])]


def block_at(part, places):
    late = [place >> 1 for place in places]
    early = [place & 1 for place in places]
    first, second, _ = ORDER[part]
    return (late[second] * 2 + late[first]) * 8 + early[0] * 4 + early[1] * 2 + early[2]


def total(arrays):
    return functools.reduce(lambda a, b: a + b, [a.astype(F32) for a in arrays])


def split3(v):
    hi = lax.reduce_precision(v, 8, 7)
    mid = lax.reduce_precision(v - hi, 8, 7)
    lo = v - hi - mid
    return [hi.astype(BF), mid.astype(BF), lo.astype(BF)]


def table(x, y, z, core, shard):
    out = []
    place = jnp.arange(4, dtype=jnp.int32)

    def swap(bits):
        return jnp.where(core == 0, bits, (bits & 1) * 2 + (bits >> 1))

    mine = [swap(c ^ (c >> 1)) & 2 for c in (x, y, z)]
    for late in mine:
        gray = swap(place ^ late)
        out.append(gray ^ (gray >> 1))
    for late in mine:
        out.append(swap(place ^ (place >> 1)) ^ late)
    out.append(jnp.stack([shard * VB, (shard ^ 1) * VB]))
    return jnp.concatenate(out).astype(jnp.int32)


def at_of(tab, dim, place):
    return tab[4 * dim + place]


def place_of(tab, dim, at):
    return tab[12 + 4 * dim + at]


def flip_kernel(own_ref, other_ref, a_ref, b_ref, c_ref):
    for h, ref in enumerate((own_ref, other_ref)):
        turned = ref[...].T
        cols = pl.ds(h * VB, VB)
        for ylo in range(2):
            at = ylo * FB
            a_ref[ylo, 0, :, cols] = turned[at : at + PT]
            b_ref[0, ylo, :, cols] = turned[at + PT : at + 2 * PT]
            c_ref[ylo, 0, :, cols] = turned[at + 2 * PT : at + 3 * PT]


def flip(own, other):
    block = pl.BlockSpec((VB, 2 * FB), lambda x: (0, x))
    return pl.pallas_call(
        flip_kernel,
        grid=(4,),
        in_specs=[block, block],
        out_specs=[
            pl.BlockSpec((2, 1, PT, 2 * VB), lambda x: (0, x, 0, 0)),
            pl.BlockSpec((1, 2, PT, 2 * VB), lambda x: (x, 0, 0, 0)),
            pl.BlockSpec((2, 1, PT, 2 * VB), lambda x: (0, x, 0, 0)),
        ],
        out_shape=[
            jax.ShapeDtypeStruct((2, 4, PT, 2 * VB), BF),
            jax.ShapeDtypeStruct((4, 2, PT, 2 * VB), BF),
            jax.ShapeDtypeStruct((2, 4, PT, 2 * VB), BF),
        ],
        compiler_params=pltpu.CompilerParams(vmem_limit_bytes=VMEM),
        cost_estimate=pl.CostEstimate(
            flops=0, bytes_accessed=4 * VB * D * 2, transcendentals=0
        ),
        name="flip",
    )(own, other)


def act_kernel(tab, *refs):
    halves = [refs[2 * p : 2 * p + 2] for p in range(3)]
    own_ref, other_ref, tgt_ref = refs[6:9]
    expo_ref, bend_ref, rinv_ref, stat_ref, xt_out = refs[9:14]
    xt, squares, weights, acc, totals, stats, sems, out_sems, w_sems = refs[14:]
    step = pl.program_id(0)

    def fetch(src, tile, x, y, part):
        row = (x * 2 + (y & 1)) * FB + part * PT
        lanes = pl.ds(pl.multiple_of((y >> 1) * TB, TB), TB)
        pltpu.make_async_copy(
            src.at[pl.ds(0, PT)],
            xt.at[tile, pl.ds(pl.multiple_of(row, 16), PT), lanes],
            sems.at[tile],
        ).start()
        if part == 0:
            row = (x * 2 + (y & 1)) * SQ
            pltpu.make_async_copy(
                src.at[pl.ds(PT, SQ)],
                squares.at[tile, pl.ds(pl.multiple_of(row, 16), SQ), lanes],
                sems.at[tile],
            ).start()

    def issue(tile):
        for px in range(4):
            for py in range(4):
                x, y = at_of(tab, 0, px), at_of(tab, 1, py)
                places = (px, py, tile)
                fetch(halves[1][px >> 1].at[block_at(1, places)], tile, x, y, 1)
                fetch(halves[2][py >> 1].at[block_at(2, places)], tile, x, y, 2)
        for half in range(2):
            @pl.when((tile >> 1) == half)
            def _():
                for px in range(4):
                    for py in range(4):
                        fetch(
                            halves[0][half].at[block_at(0, (px, py, tile))],
                            tile, at_of(tab, 0, px), at_of(tab, 1, py), 0,
                        )

    def load(h, ref):
        return pltpu.make_async_copy(ref, weights.at[pl.ds(h * VB, VB)], w_sems.at[h])

    def arrived():
        pltpu.make_async_copy(xt.at[step], xt.at[step], sems.at[step]).wait()
        pltpu.make_async_copy(squares.at[step], squares.at[step], sems.at[step]).wait()
        pltpu.make_async_copy(xt.at[step], xt_out.at[step], out_sems.at[step]).start()

    @pl.when(step == 0)
    def _():
        issue(step)
        for h, ref in enumerate((own_ref, other_ref)):
            load(h, ref).start()
        issue(step + 1)
        arrived()
        for h, ref in enumerate((own_ref, other_ref)):
            load(h, ref).wait()
            rows = pl.ds(h * VB, VB)
            acc[rows, :] = jnp.dot(weights[rows, :], xt[step], preferred_element_type=F32)

    @pl.when(step > 0)
    def _():
        @pl.when(step < 3)
        def _():
            issue(step + 1)

        arrived()
        acc[...] = jnp.dot(weights[...], xt[step], preferred_element_type=F32)

    mean = jnp.sum(squares[step].astype(F32), axis=0, keepdims=True) / D
    rinv = lax.rsqrt(mean + EPS)
    z = at_of(tab, 2, step)
    rinv_ref[z] = rinv
    tgt = tgt_ref[z]
    rows = 32
    zeros = jnp.zeros((8, 2 * TB), F32)
    sums = (zeros,) * 3
    inside = jnp.zeros((1, 2 * TB), jnp.bool_)

    def fold(v):
        return jnp.sum(v.reshape(rows // 8, 8, 2 * TB), axis=0)

    for h in range(2):
        row0 = lax.broadcasted_iota(jnp.int32, (rows, 2 * TB), 0) + tab[24 + h]
        inside = inside | ((tgt >= tab[24 + h]) & (tgt < tab[24 + h] + VB))

        def chunk(i, sums, h=h, row0=row0):
            total, slope, act_at = sums
            at = pl.multiple_of(i * rows, rows)
            here = pl.ds(h * VB + at, rows)
            act = acc[here, :] * rinv
            t = jnp.tanh(act * (1.0 / CAP))
            expo = jnp.exp(t * CAP)
            sharp = expo * (1.0 - t * t)
            expo_ref[0, here, :] = sharp
            return (
                total + fold(expo),
                slope + fold(sharp * act),
                act_at + fold(jnp.where(row0 + at == tgt, act, 0.0)),
            )

        sums = lax.fori_loop(0, VB // rows, chunk, sums)
    total, slope, act_at = [jnp.sum(s, axis=0, keepdims=True) for s in sums]
    t = jnp.tanh(act_at * (1.0 / CAP))
    bend = jnp.where(inside, 1.0 - t * t, 0.0)
    bend_ref[0] = bend
    sums = (total, t * CAP, slope, bend * act_at)
    for yhi in range(2):
        lanes = slice(yhi * TB, (yhi + 1) * TB)
        totals[pl.ds(z * 2 + yhi, 1), :] = sums[0][:, lanes]
        stats[yhi * 4 + z] = jnp.concatenate(
            [s[:, lanes] for s in sums[1:4]] + [jnp.zeros((5, TB), F32)], axis=0
        )

    @pl.when(step == 3)
    def _():
        for chip in range(64):
            stat_ref[chip, 0:8, :] = totals[...]
            stat_ref[chip, 8:16, :] = stats[chip % 8]
        for tile in range(4):
            pltpu.make_async_copy(xt.at[tile], xt_out.at[tile], out_sems.at[tile]).wait()


ANYWHERE = pl.BlockSpec(memory_space=pl.ANY)
SMEM_SPEC = pl.BlockSpec(memory_space=pltpu.SMEM)
VMEM_SPEC = pl.BlockSpec(memory_space=pltpu.VMEM)


def act_call(tab, halves, own, other, tgt):
    tile = pl.BlockSpec((1, 2 * VB, 2 * TB), lambda z, w: (z, 0, 0))
    rows = pl.BlockSpec((4, 1, 2 * TB), lambda z, w: (0, 0, 0))
    return pl.pallas_call(
        act_kernel,
        grid_spec=pltpu.PrefetchScalarGridSpec(
            num_scalar_prefetch=1,
            grid=(4,),
            in_specs=[ANYWHERE] * 8 + [rows],
            out_specs=[
                tile,
                pl.BlockSpec((1, 1, 2 * TB), lambda z, w: (z, 0, 0)),
                rows,
                pl.BlockSpec((64, 16, TB), lambda z, w: (0, 0, 0)),
                ANYWHERE,
            ],
            scratch_shapes=[
                pltpu.VMEM((4, D, 2 * TB), BF),
                pltpu.VMEM((4, 8 * SQ, 2 * TB), BF),
                pltpu.VMEM((2 * VB, D), BF),
                pltpu.VMEM((2 * VB, 2 * TB), F32),
                pltpu.VMEM((8, TB), F32),
                pltpu.VMEM((8, 8, TB), F32),
                pltpu.SemaphoreType.DMA((4,)),
                pltpu.SemaphoreType.DMA((4,)),
                pltpu.SemaphoreType.DMA((2,)),
            ],
        ),
        out_shape=[
            jax.ShapeDtypeStruct((4, 2 * VB, 2 * TB), F32),
            jax.ShapeDtypeStruct((4, 1, 2 * TB), F32),
            jax.ShapeDtypeStruct((4, 1, 2 * TB), F32),
            jax.ShapeDtypeStruct((64, 16, TB), F32),
            jax.ShapeDtypeStruct((4, D, 2 * TB), BF),
        ],
        compiler_params=pltpu.CompilerParams(vmem_limit_bytes=VMEM),
        cost_estimate=pl.CostEstimate(
            flops=2 * 1024 * 1024 * D, bytes_accessed=30_000_000, transcendentals=2 << 20
        ),
        name="act",
    )(tab, *halves, own, other, tgt)


def pieces(tab, lead, gz, gy, weights, outs, ready, done):
    w0, w1, w2 = weights
    out0, out1, out2 = outs
    ready(0)
    w = w0[...].reshape(8 * PT, 2 * VB)
    both = jnp.concatenate([gz[lead * 2], gz[lead * 2 + 1]], axis=1)
    got = jnp.dot(w, both, preferred_element_type=F32).astype(BF)
    for low in range(2):
        for x in range(4):
            for ylo in range(2):
                for yhi in range(2):
                    places = (place_of(tab, 0, x), place_of(tab, 1, yhi * 2 + ylo), lead * 2 + low)
                    row, lane = (ylo * 4 + x) * PT, (low * 2 + yhi) * TB
                    out0[block_at(0, places)] = got[row : row + PT, lane : lane + TB]
    done(0)
    ready(1)
    for low in range(2):
        place = lead * 2 + low
        x = at_of(tab, 0, place)
        w = w1[x].reshape(2 * PT, 2 * VB)
        tokens = jnp.concatenate([gz[z] for z in range(4)], axis=1)
        got = jnp.dot(w, tokens, preferred_element_type=F32).astype(BF)
        for z in range(4):
            for ylo in range(2):
                for yhi in range(2):
                    places = (place, place_of(tab, 1, yhi * 2 + ylo), z)
                    row, lane = ylo * PT, (z * 2 + yhi) * TB
                    out1[block_at(1, places)] = got[row : row + PT, lane : lane + TB]
    done(1)
    ready(2)
    for low in range(2):
        place = lead * 2 + low
        y = at_of(tab, 1, place)
        w = w2[y & 1].reshape(4 * PT, 2 * VB)
        tokens = jnp.concatenate([gy[y >> 1, pair] for pair in range(2)], axis=1)
        got = jnp.dot(w, tokens, preferred_element_type=F32).astype(BF)
        for x in range(4):
            for z in range(4):
                places = (place_of(tab, 0, x), place, z)
                out2[block_at(2, places)] = got[x * PT : (x + 1) * PT, z * TB : (z + 1) * TB]
    done(2)


def copies(pairs, sems):
    return [
        pltpu.make_async_copy(src, dst, sems.at[i]) for i, (src, dst) in enumerate(pairs)
    ]


def grad_kernel(tab, expo_ref, bend_ref, totals_ref, rinv_ref, tgt_ref, *refs):
    w_refs, out_refs = refs[:3], refs[3:10]
    expo, w0, w1, w2, gz, gr, gy, away0, away1, away2, in_sems, out_sems = refs[10:]
    weights, away = (w0, w1, w2), (away0, away1, away2)
    tiles = [(expo_ref.at[i], expo.at[i]) for i in range(4)]
    incoming = copies(tiles + list(zip(w_refs, weights)), in_sems)
    by_rows = (gr.at[:, pl.ds(0, VB)], gr.at[:, pl.ds(VB, VB)])
    outgoing = copies(list(zip(by_rows + (gz, gy) + away, out_refs)), out_sems)
    for copy in incoming:
        copy.start()
    rows = 32
    inv = 1.0 / jnp.sum(totals_ref[...], axis=0)[0:8]
    line = lax.broadcasted_iota(jnp.int32, (8, TB), 0)

    def chunk(i, carry, place, h, inv_z, rinv, bend, tgt, row0):
        at = pl.multiple_of(i * rows, rows)
        here = pl.ds(h * VB + at, rows)
        g = expo[place, here, :] * inv_z - jnp.where(row0 + at == tgt, bend, 0.0)
        gr[place, here, :] = (g * rinv).astype(BF)
        g = g.astype(BF)
        gz[place, here, :] = g
        for yhi in range(2):
            gy[yhi, place // 2, here, pl.ds(place % 2 * TB, TB)] = g[:, yhi * TB : (yhi + 1) * TB]
        return carry

    for place in range(4):
        z = at_of(tab, 2, place)
        inv_z = jnp.concatenate(
            [
                jnp.sum(jnp.where(line == z * 2 + yhi, inv, 0.0), axis=0, keepdims=True)
                for yhi in range(2)
            ],
            axis=1,
        )
        incoming[place].wait()
        for h in range(2):
            row0 = lax.broadcasted_iota(jnp.int32, (rows, 2 * TB), 0) + tab[24 + h]
            lax.fori_loop(
                0,
                VB // rows,
                functools.partial(
                    chunk, place=place, h=h, inv_z=inv_z, rinv=rinv_ref[z],
                    bend=bend_ref[place], tgt=tgt_ref[z], row0=row0,
                ),
                0,
            )
    for copy in outgoing[:4]:
        copy.start()
    pieces(
        tab, 1, gz, gy, weights, away,
        lambda p: incoming[4 + p].wait(), lambda p: outgoing[4 + p].start(),
    )
    for copy in outgoing:
        copy.wait()


def keep_kernel(tab, gz_ref, gy_ref, *refs):
    w_refs, out_refs = refs[:3], refs[3:6]
    gz, w0, w1, gy, w2, kept0, kept1, kept2, in_sems, out_sems = refs[6:]
    kept = (kept0, kept1, kept2)
    incoming = copies(
        [(gz_ref, gz), (w_refs[0], w0), (w_refs[1], w1), (gy_ref, gy), (w_refs[2], w2)], in_sems
    )
    outgoing = copies(list(zip(kept, out_refs)), out_sems)
    for copy in incoming:
        copy.start()

    def ready(p):
        for copy in ((0, 1), (2,), (3, 4))[p]:
            incoming[copy].wait()

    pieces(tab, 0, gz, gy, (w0, w1, w2), kept, ready, lambda p: outgoing[p].start())
    for copy in outgoing:
        copy.wait()


HALF = (32, PT, TB)
GZ = (4, 2 * VB, 2 * TB)
GR = (4, VB, 2 * TB)
GY = (2, 2, 2 * VB, 2 * TB)
W_SHAPES = ((2, 4, PT, 2 * VB), (4, 2, PT, 2 * VB), (2, 4, PT, 2 * VB))


def bf16_out(*shapes):
    return [jax.ShapeDtypeStruct(shape, BF) for shape in shapes]


def bf16_vmem(*shapes):
    return [pltpu.VMEM(shape, BF) for shape in shapes]


def grad_call(tab, expo, bend, totals, rinv, tgt, turned):
    return pl.pallas_call(
        grad_kernel,
        in_specs=[SMEM_SPEC, ANYWHERE] + [VMEM_SPEC] * 4 + [ANYWHERE] * 3,
        out_specs=[ANYWHERE] * 7,
        out_shape=bf16_out(GR, GR, GZ, GY, HALF, HALF, HALF),
        scratch_shapes=[pltpu.VMEM(GZ, F32)]
        + bf16_vmem(*W_SHAPES, GZ, GZ, GY, HALF, HALF, HALF)
        + [pltpu.SemaphoreType.DMA((7,)), pltpu.SemaphoreType.DMA((7,))],
        compiler_params=pltpu.CompilerParams(vmem_limit_bytes=VMEM),
        cost_estimate=pl.CostEstimate(
            flops=1024 * 1024 * D, bytes_accessed=24_000_000, transcendentals=0
        ),
        name="grad",
    )(tab, expo, bend, totals, rinv, tgt, *turned)


def keep_call(tab, gz, gy, turned):
    return pl.pallas_call(
        keep_kernel,
        in_specs=[SMEM_SPEC] + [ANYWHERE] * 5,
        out_specs=[ANYWHERE] * 3,
        out_shape=bf16_out(HALF, HALF, HALF),
        scratch_shapes=bf16_vmem(
            GZ, W_SHAPES[0], W_SHAPES[1], GY, W_SHAPES[2], HALF, HALF, HALF
        )
        + [pltpu.SemaphoreType.DMA((5,)), pltpu.SemaphoreType.DMA((3,))],
        compiler_params=pltpu.CompilerParams(vmem_limit_bytes=VMEM),
        cost_estimate=pl.CostEstimate(
            flops=1024 * D, bytes_accessed=1_000_000, transcendentals=0
        ),
        name="keep",
    )(tab, gz, gy, *turned)


def head_kernel(own_gr, twin_gr, own_xt, twin_xt, w, *refs):
    head_ref, gain_ref = refs[-2:]
    got = lax.dot_general(
        jnp.concatenate([gr[z] for gr in (own_gr, twin_gr) for z in range(4)], axis=1),
        jnp.concatenate([xt[z] for xt in (own_xt, twin_xt) for z in range(4)], axis=1),
        (((1,), (1,)), ((), ())), preferred_element_type=F32,
    )
    head_ref[...] = got.astype(BF)
    gain = jnp.sum(got * w[...].astype(F32), axis=0, keepdims=True)
    for i in range(gain_ref.shape[1]):
        gain_ref[0, i : i + 1, :] = gain[:, i * TB : (i + 1) * TB]


TILE = 768


def head_call(grs, xts, w, first, count, held=()):
    cols = pl.BlockSpec((VB, TILE), lambda f: (0, f + first))
    rows = pl.BlockSpec(GR, lambda f: (0, 0, 0), pipeline_mode=pl.Buffered(1))
    tokens = pl.BlockSpec((4, TILE, 2 * TB), lambda f: (0, f + first, 0))
    return pl.pallas_call(
        head_kernel,
        grid=(count,),
        in_specs=[rows, rows, tokens, tokens, cols] + [ANYWHERE] * len(held),
        out_specs=[cols, pl.BlockSpec((1, TILE // TB, TB), lambda f: (f, 0, 0))],
        out_shape=bf16_out((VB, D)) + [jax.ShapeDtypeStruct((count, TILE // TB, TB), F32)],
        input_output_aliases={5 + i: i for i in range(len(held))},
        compiler_params=pltpu.CompilerParams(vmem_limit_bytes=VMEM),
        cost_estimate=pl.CostEstimate(
            flops=1024 * D, bytes_accessed=1_000_000, transcendentals=0
        ),
        name="head",
    )(*grs, *xts, w, *held)


def sum_kernel(terms, *refs):
    ins, outs = refs[: 3 * terms], refs[3 * terms :]
    for p in range(3):
        blocks = [a[...] for a in ins[terms * p : terms * (p + 1)]]
        got = blocks[0] + blocks[1] if terms == 2 else total(blocks).astype(BF)
        if len(outs) == 3:
            outs[p][...] = got
        else:
            outs[-1][:, p * PT : (p + 1) * PT, :] = got
    if len(outs) == 2:
        outs[-1][:, FB : FB + SQ, :] = outs[0][...]


def sum_call(here, count, gains=None):
    step = count // 2
    terms = len(here[0])
    specs = [
        pl.BlockSpec((step, PT, TB), lambda i, first=first // step: (i + first, 0, 0))
        for part in here
        for _, first in part
    ]
    arrays = [a for part in here for a, _ in part]
    if gains is None:
        out_specs = [pl.BlockSpec((step, PT, TB), lambda i: (i, 0, 0))] * 3
        out_shape = bf16_out(*[(count, PT, TB)] * 3)
    else:
        specs.append(pl.BlockSpec((step, SQ, TB), lambda i: (i, 0, 0)))
        arrays.append(gains)
        out_specs = pl.BlockSpec((step, FB + SQ, TB), lambda i: (i, 0, 0))
        out_shape = bf16_out((count, FB + SQ, TB))[0]
    return pl.pallas_call(
        functools.partial(sum_kernel, terms),
        grid=(count // step,),
        in_specs=specs,
        out_specs=out_specs,
        out_shape=out_shape,
        compiler_params=pltpu.CompilerParams(vmem_limit_bytes=VMEM),
        cost_estimate=pl.CostEstimate(flops=4 << 20, bytes_accessed=6_000_000, transcendentals=0),
        name="sum%d" % terms,
    )(*arrays)


def shards(section_output, norm_gain, head_weight, targets):
    x, ylo, yhi, z, core = (lax.axis_index(a) for a in AX)
    y = yhi * 2 + ylo
    shard = (((x * 2 + ylo) * 2 + yhi) * 4 + z) * 2 + core
    tab = table(x, y, z, core, shard)

    xt = section_output.T.astype(F32)
    gain = norm_gain.astype(F32)[:, None]
    scaled_x = (xt * gain).astype(BF)
    squares = jnp.sum(xt * xt, axis=0, keepdims=True)
    extra = jnp.concatenate(
        split3(squares) + [jnp.zeros((SQ - 3, TB), BF)], axis=0
    )
    block = jnp.concatenate([scaled_x[:PT], extra, scaled_x[PT:]], axis=0)
    other = send(head_weight, TWIN)
    turned = flip(head_weight, other)

    tgt = lax.dynamic_index_in_dim(
        targets.reshape(2, 4, 2, TB), core, axis=2, keepdims=False
    ).transpose(1, 0, 2).reshape(4, 1, 2 * TB)
    halves = gather(block)
    owner = jnp.stack([tab[ex] * 2 + (tab[4 + ey] & 1) for ex, ey, _ in BITS])
    owner = (owner[:, None, None] == jnp.arange(8, dtype=jnp.int32)[None, :, None]).astype(F32)
    halves, turned, tgt, tab, owner = lax.optimization_barrier((halves, turned, tgt, tab, owner))

    expo, bend, rinv, stats, xt_all = act_call(tab, halves, head_weight, other, tgt)
    xts = (xt_all, send(xt_all, TWIN))
    stats = lax.all_to_all(stats, AX[:4], 0, 0)

    own_gr, other_gr, gz, gy, *away = grad_call(tab, expo, bend, stats, rinv, tgt, turned)

    bound = lax.optimization_barrier

    def exchange(away, phase):
        return [send(away[p], across(ORDER[p][phase])) for p in range(3)]

    got1 = exchange(away, 2)
    grs = (own_gr, send(other_gr, TWIN))
    kept = keep_call(tab, gz, gy, turned)
    kept, grs = bound((kept, grs))
    head_grad, gain0 = head_call(grs, xts, head_weight, 0, 4)
    got1, kept, grs, head_grad, gain0 = bound((got1, kept, grs, head_grad, gain0))
    away = sum_call([[(kept[p], 16), (got1[p], 16)] for p in range(3)], 16)

    away, grs, head_grad = bound((away, grs, head_grad))
    got2 = exchange(away, 1)
    head_grad, gain1 = head_call(grs, xts, head_weight, 4, 2, (head_grad,))
    gains = jnp.concatenate([gain0, gain1])
    gains = gains + send(gains, across(1))
    got2, gains = bound((got2, gains))
    more = send(gains, across(0))
    away = sum_call([[(kept[p], 8), (got1[p], 8), (got2[p], 8)] for p in range(3)], 8)

    away, more, gains = bound((away, more, gains))
    got3 = exchange(away, 0)
    gains = gains + more
    more = send(gains, across(2))
    got3, more = bound((got3, more))
    gains = gains + more
    here = [[(a[p], 0) for a in (kept, got1, got2, got3)] for p in range(3)]

    gains = jnp.sum(owner * gains.reshape(1, 8, FB), axis=1)
    gains = jnp.concatenate([gains, jnp.zeros((8, 5 * TB - FB), F32)], axis=1)
    gains = jnp.stack(split3(gains) + [jnp.zeros((8, 5 * TB), BF)], axis=1)
    gains = gains.reshape(8, 20, TB)[:, :SQ]

    blocks = in_cube(sum_call(here, 8, gains))
    blocks = jnp.sum(blocks.astype(F32), axis=0)
    grad_hidden = blocks[:FB]
    gains = jnp.sum(blocks[FB : FB + 15].reshape(3, 5 * TB), axis=0)[:FB]
    gain_grad = (gains + send(gains, TWIN)) / norm_gain.astype(F32)

    row = jnp.sum(stats, axis=0)
    picked, slope, slope_at = row[8:9], row[9:10], row[10:11]
    sum_exp = lax.dynamic_slice(row, (z * 2 + yhi, 0), (1, TB))
    rinv = lax.dynamic_slice(rinv, (z, 0, yhi * TB), (1, 1, TB)).reshape(1, TB)
    token_loss = (jnp.log(sum_exp) - picked).reshape(TB)
    inner = slope / sum_exp - slope_at
    grad_input = (rinv * (grad_hidden * gain) - xt * (rinv * rinv * inner / D)).astype(BF).T
    return (token_loss, grad_input, head_grad, gain_grad)


def solution(mesh):
    fine = Mesh(mesh.devices.reshape(4, 2, 2, 4, 2), AX)
    pipe, dp = ("x", "ylo"), ("yhi", "z", "core")
    return jax.shard_map(
        shards,
        mesh=fine,
        in_specs=(P(dp, pipe), P(pipe), P(pipe + dp, None), P()),
        out_specs=(P(dp), P(dp, pipe), P(pipe + dp, None), P(pipe)),
        check_vma=False,
    )
```

```python
import functools
import itertools

import jax
import jax.numpy as jnp
import numpy as np
from jax import lax
from jax.experimental import pallas as pl
from jax.experimental.pallas import tpu as pltpu
from jax.sharding import Mesh, PartitionSpec as P

AX = ("x", "ylo", "yhi", "z", "core")
D = 4608
FB = 576
PT = 192
SQ = 16
TB = 128
VB = 512
CAP = 30.0
EPS = 1e-06
VMEM = 60 * 1024 * 1024
BF = jnp.bfloat16
F32 = jnp.float32

ORDER = ((0, 1, 2), (1, 2, 0), (2, 0, 1))


def coords(i):
    core, z, yhi, ylo, x = i % 2, i // 2 % 4, i // 8 % 2, i // 16 % 2, i // 32
    return [x, yhi * 2 + ylo, z], core


def number(c, core):
    return (((c[0] * 2 + c[1] % 2) * 2 + c[1] // 2) * 4 + c[2]) * 2 + core


def from_bits(core, late, early):
    gray = late * 2 + early if core == 0 else early * 2 + late
    return gray ^ (gray >> 1)


BITS = list(itertools.product((0, 1), repeat=3))
CUBES = [
    [number([from_bits(core, b, e) for b, e in zip(late, early)], core) for early in BITS]
    for core in (0, 1)
    for late in BITS
]
TWIN = [(i, i ^ 1) for i in range(128)]


@functools.cache
def across(dim):
    pairs = []
    for i in range(128):
        c, core = coords(i)
        gray = (c[dim] ^ (c[dim] >> 1)) ^ (2 if core == 0 else 1)
        c[dim] = gray ^ (gray >> 1)
        pairs.append((i, number(c, core)))
    return pairs


def send(a, pairs):
    return lax.ppermute(a, AX, pairs)


def in_cube(a):
    return lax.all_to_all(a, AX, 0, 0, axis_index_groups=CUBES)


def gather(block):
    cube = in_cube(jnp.broadcast_to(block[None], (8,) + block.shape))
    cuts = (0, PT + SQ, 2 * PT + SQ, 3 * PT + SQ)
    held = [cube[:, cuts[p] : cuts[p + 1]] for p in range(3)]
    for phase in range(2):
        got = [send(held[p], across(ORDER[p][phase])) for p in range(3)]
        held = [jnp.concatenate([held[p], got[p]]) for p in range(3)]
    got = [send(held[p], across(ORDER[p][2])) for p in range(3)]
    return [a for p in range(3) for a in (held[p], got[p])]


def block_at(part, places):
    late = [place >> 1 for place in places]
    early = [place & 1 for place in places]
    first, second, _ = ORDER[part]
    return (late[second] * 2 + late[first]) * 8 + early[0] * 4 + early[1] * 2 + early[2]


def split3(v):
    hi = lax.reduce_precision(v, 8, 7)
    mid = lax.reduce_precision(v - hi, 8, 7)
    lo = v - hi - mid
    return [hi.astype(BF), mid.astype(BF), lo.astype(BF)]


def table(x, y, z, core, shard):
    out = []
    place = jnp.arange(4, dtype=jnp.int32)

    def swap(bits):
        return jnp.where(core == 0, bits, (bits & 1) * 2 + (bits >> 1))

    mine = [swap(c ^ (c >> 1)) & 2 for c in (x, y, z)]
    for late in mine:
        gray = swap(place ^ late)
        out.append(gray ^ (gray >> 1))
    for late in mine:
        out.append(swap(place ^ (place >> 1)) ^ late)
    out.append(jnp.stack([shard * VB, (shard ^ 1) * VB]))
    return jnp.concatenate(out).astype(jnp.int32)


def at_of(tab, dim, place):
    return tab[4 * dim + place]


def place_of(tab, dim, at):
    return tab[12 + 4 * dim + at]


def flip_kernel(own_ref, other_ref, a_ref, b_ref, c_ref):
    for h, ref in enumerate((own_ref, other_ref)):
        turned = ref[...].T
        cols = pl.ds(h * VB, VB)
        for ylo in range(2):
            at = ylo * FB
            a_ref[ylo, 0, :, cols] = turned[at : at + PT]
            b_ref[0, ylo, :, cols] = turned[at + PT : at + 2 * PT]
            c_ref[ylo, 0, :, cols] = turned[at + 2 * PT : at + 3 * PT]


def flip(own, other):
    block = pl.BlockSpec((VB, 2 * FB), lambda x: (0, x))
    return pl.pallas_call(
        flip_kernel,
        grid=(4,),
        in_specs=[block, block],
        out_specs=[
            pl.BlockSpec((2, 1, PT, 2 * VB), lambda x: (0, x, 0, 0)),
            pl.BlockSpec((1, 2, PT, 2 * VB), lambda x: (x, 0, 0, 0)),
            pl.BlockSpec((2, 1, PT, 2 * VB), lambda x: (0, x, 0, 0)),
        ],
        out_shape=[
            jax.ShapeDtypeStruct((2, 4, PT, 2 * VB), BF),
            jax.ShapeDtypeStruct((4, 2, PT, 2 * VB), BF),
            jax.ShapeDtypeStruct((2, 4, PT, 2 * VB), BF),
        ],
        compiler_params=pltpu.CompilerParams(vmem_limit_bytes=VMEM),
        cost_estimate=pl.CostEstimate(
            flops=0, bytes_accessed=4 * VB * D * 2, transcendentals=0
        ),
        name="flip",
    )(own, other)


def act_kernel(tab, *refs):
    halves = [refs[2 * p : 2 * p + 2] for p in range(3)]
    own_ref, other_ref, tgt_ref = refs[6:9]
    expo_ref, bend_ref, rinv_ref, stat_ref, xt_out = refs[9:14]
    xt, squares, weights, acc, totals, stats, sems, out_sems, w_sems = refs[14:]
    step = pl.program_id(0)

    def fetch(src, tile, x, y, part):
        row = (x * 2 + (y & 1)) * FB + part * PT
        lanes = pl.ds(pl.multiple_of((y >> 1) * TB, TB), TB)
        pltpu.make_async_copy(
            src.at[pl.ds(0, PT)],
            xt.at[tile, pl.ds(pl.multiple_of(row, 16), PT), lanes],
            sems.at[tile],
        ).start()
        if part == 0:
            row = (x * 2 + (y & 1)) * SQ
            pltpu.make_async_copy(
                src.at[pl.ds(PT, SQ)],
                squares.at[tile, pl.ds(pl.multiple_of(row, 16), SQ), lanes],
                sems.at[tile],
            ).start()

    def issue(tile):
        for px in range(4):
            for py in range(4):
                x, y = at_of(tab, 0, px), at_of(tab, 1, py)
                places = (px, py, tile)
                fetch(halves[1][px >> 1].at[block_at(1, places)], tile, x, y, 1)
                fetch(halves[2][py >> 1].at[block_at(2, places)], tile, x, y, 2)
        for half in range(2):
            @pl.when((tile >> 1) == half)
            def _():
                for px in range(4):
                    for py in range(4):
                        fetch(
                            halves[0][half].at[block_at(0, (px, py, tile))],
                            tile, at_of(tab, 0, px), at_of(tab, 1, py), 0,
                        )

    def load(h, ref):
        return pltpu.make_async_copy(ref, weights.at[pl.ds(h * VB, VB)], w_sems.at[h])

    def arrived():
        pltpu.make_async_copy(xt.at[step], xt.at[step], sems.at[step]).wait()
        pltpu.make_async_copy(squares.at[step], squares.at[step], sems.at[step]).wait()
        pltpu.make_async_copy(xt.at[step], xt_out.at[step], out_sems.at[step]).start()

    @pl.when(step == 0)
    def _():
        issue(step)
        for h, ref in enumerate((own_ref, other_ref)):
            load(h, ref).start()
        issue(step + 1)
        arrived()
        for h, ref in enumerate((own_ref, other_ref)):
            load(h, ref).wait()
            rows = pl.ds(h * VB, VB)
            acc[rows, :] = jnp.dot(weights[rows, :], xt[step], preferred_element_type=F32)

    @pl.when(step > 0)
    def _():
        @pl.when(step < 3)
        def _():
            issue(step + 1)

        arrived()
        acc[...] = jnp.dot(weights[...], xt[step], preferred_element_type=F32)

    mean = jnp.sum(squares[step].astype(F32), axis=0, keepdims=True) / D
    rinv = lax.rsqrt(mean + EPS)
    z = at_of(tab, 2, step)
    rinv_ref[z] = rinv
    tgt = tgt_ref[z]
    rows = 64
    zeros = jnp.zeros((8, 2 * TB), F32)
    sums = (zeros,) * 3
    inside = jnp.zeros((1, 2 * TB), jnp.bool_)

    def fold(v):
        return jnp.sum(v.reshape(rows // 8, 8, 2 * TB), axis=0)

    for h in range(2):
        row0 = lax.broadcasted_iota(jnp.int32, (rows, 2 * TB), 0) + tab[24 + h]
        inside = inside | ((tgt >= tab[24 + h]) & (tgt < tab[24 + h] + VB))

        def chunk(i, sums, h=h, row0=row0):
            total, slope, act_at = sums
            at = pl.multiple_of(i * rows, rows)
            here = pl.ds(h * VB + at, rows)
            act = acc[here, :] * rinv
            t = jnp.tanh(act * (1.0 / CAP))
            expo = jnp.exp(t * CAP)
            sharp = expo * (1.0 - t * t)
            expo_ref[0, here, :] = sharp
            return (
                total + fold(expo),
                slope + fold(sharp * act),
                act_at + fold(jnp.where(row0 + at == tgt, act, 0.0)),
            )

        sums = lax.fori_loop(0, VB // rows, chunk, sums)
    total, slope, act_at = [jnp.sum(s, axis=0, keepdims=True) for s in sums]
    t = jnp.tanh(act_at * (1.0 / CAP))
    bend = jnp.where(inside, 1.0 - t * t, 0.0)
    bend_ref[0] = bend
    sums = (total, t * CAP, slope, bend * act_at)
    for yhi in range(2):
        lanes = slice(yhi * TB, (yhi + 1) * TB)
        totals[pl.ds(z * 2 + yhi, 1), :] = sums[0][:, lanes]
        stats[yhi * 4 + z] = jnp.concatenate(
            [s[:, lanes] for s in sums[1:4]] + [jnp.zeros((5, TB), F32)], axis=0
        )

    @pl.when(step == 3)
    def _():
        for chip in range(64):
            stat_ref[chip, 0:8, :] = totals[...]
            stat_ref[chip, 8:16, :] = stats[chip % 8]
        for tile in range(4):
            pltpu.make_async_copy(xt.at[tile], xt_out.at[tile], out_sems.at[tile]).wait()


ANYWHERE = pl.BlockSpec(memory_space=pl.ANY)
SMEM_SPEC = pl.BlockSpec(memory_space=pltpu.SMEM)
VMEM_SPEC = pl.BlockSpec(memory_space=pltpu.VMEM)


def act_call(tab, halves, own, other, tgt):
    tile = pl.BlockSpec((1, 2 * VB, 2 * TB), lambda z, w: (z, 0, 0))
    rows = pl.BlockSpec((4, 1, 2 * TB), lambda z, w: (0, 0, 0))
    return pl.pallas_call(
        act_kernel,
        grid_spec=pltpu.PrefetchScalarGridSpec(
            num_scalar_prefetch=1,
            grid=(4,),
            in_specs=[ANYWHERE] * 8 + [rows],
            out_specs=[
                tile,
                pl.BlockSpec((1, 1, 2 * TB), lambda z, w: (z, 0, 0)),
                rows,
                pl.BlockSpec((64, 16, TB), lambda z, w: (0, 0, 0)),
                ANYWHERE,
            ],
            scratch_shapes=[
                pltpu.VMEM((4, D, 2 * TB), BF),
                pltpu.VMEM((4, 8 * SQ, 2 * TB), BF),
                pltpu.VMEM((2 * VB, D), BF),
                pltpu.VMEM((2 * VB, 2 * TB), F32),
                pltpu.VMEM((8, TB), F32),
                pltpu.VMEM((8, 8, TB), F32),
                pltpu.SemaphoreType.DMA((4,)),
                pltpu.SemaphoreType.DMA((4,)),
                pltpu.SemaphoreType.DMA((2,)),
            ],
        ),
        out_shape=[
            jax.ShapeDtypeStruct((4, 2 * VB, 2 * TB), F32),
            jax.ShapeDtypeStruct((4, 1, 2 * TB), F32),
            jax.ShapeDtypeStruct((4, 1, 2 * TB), F32),
            jax.ShapeDtypeStruct((64, 16, TB), F32),
            jax.ShapeDtypeStruct((4, D, 2 * TB), BF),
        ],
        compiler_params=pltpu.CompilerParams(vmem_limit_bytes=VMEM),
        cost_estimate=pl.CostEstimate(
            flops=2 * 1024 * 1024 * D, bytes_accessed=30_000_000, transcendentals=2 << 20
        ),
        name="act",
    )(tab, *halves, own, other, tgt)


def pieces(tab, lead, gz, gy, weights, outs, ready, done):
    w0, w1, w2 = weights
    out0, out1, out2 = outs
    ready(0)
    w = w0[...].reshape(8 * PT, 2 * VB)
    both = jnp.concatenate([gz[lead * 2], gz[lead * 2 + 1]], axis=1)
    got = jnp.dot(w, both, preferred_element_type=F32).astype(BF)
    for low in range(2):
        for x in range(4):
            for ylo in range(2):
                for yhi in range(2):
                    places = (place_of(tab, 0, x), place_of(tab, 1, yhi * 2 + ylo), lead * 2 + low)
                    row, lane = (ylo * 4 + x) * PT, (low * 2 + yhi) * TB
                    out0[block_at(0, places)] = got[row : row + PT, lane : lane + TB]
    done(0)
    ready(1)
    for low in range(2):
        place = lead * 2 + low
        x = at_of(tab, 0, place)
        w = w1[x].reshape(2 * PT, 2 * VB)
        tokens = jnp.concatenate([gz[z] for z in range(4)], axis=1)
        got = jnp.dot(w, tokens, preferred_element_type=F32).astype(BF)
        for z in range(4):
            for ylo in range(2):
                for yhi in range(2):
                    places = (place, place_of(tab, 1, yhi * 2 + ylo), z)
                    row, lane = ylo * PT, (z * 2 + yhi) * TB
                    out1[block_at(1, places)] = got[row : row + PT, lane : lane + TB]
    done(1)
    ready(2)
    for low in range(2):
        place = lead * 2 + low
        y = at_of(tab, 1, place)
        w = w2[y & 1].reshape(4 * PT, 2 * VB)
        tokens = jnp.concatenate([gy[y >> 1, pair] for pair in range(2)], axis=1)
        got = jnp.dot(w, tokens, preferred_element_type=F32).astype(BF)
        for x in range(4):
            for z in range(4):
                places = (place_of(tab, 0, x), place, z)
                out2[block_at(2, places)] = got[x * PT : (x + 1) * PT, z * TB : (z + 1) * TB]
    done(2)


def copies(pairs, sems):
    return [
        pltpu.make_async_copy(src, dst, sems.at[i]) for i, (src, dst) in enumerate(pairs)
    ]


def grad_kernel(tab, expo_ref, bend_ref, totals_ref, rinv_ref, tgt_ref, *refs):
    w_refs, out_refs = refs[:3], refs[3:10]
    expo, w0, w1, w2, gz, gr, gy, away0, away1, away2, in_sems, out_sems = refs[10:]
    weights, away = (w0, w1, w2), (away0, away1, away2)
    tiles = [(expo_ref.at[i], expo.at[i]) for i in range(4)]
    incoming = copies(tiles + list(zip(w_refs, weights)), in_sems)
    by_rows = (gr.at[:, pl.ds(0, VB)], gr.at[:, pl.ds(VB, VB)])
    outgoing = copies(list(zip(by_rows + (gz, gy) + away, out_refs)), out_sems)
    for copy in incoming:
        copy.start()
    rows = 32
    inv = 1.0 / jnp.sum(totals_ref[...], axis=0)[0:8]
    line = lax.broadcasted_iota(jnp.int32, (8, TB), 0)

    def chunk(i, carry, place, h, inv_z, rinv, bend, tgt, row0):
        at = pl.multiple_of(i * rows, rows)
        here = pl.ds(h * VB + at, rows)
        g = expo[place, here, :] * inv_z - jnp.where(row0 + at == tgt, bend, 0.0)
        gr[place, here, :] = (g * rinv).astype(BF)
        g = g.astype(BF)
        gz[place, here, :] = g
        for yhi in range(2):
            gy[yhi, place // 2, here, pl.ds(place % 2 * TB, TB)] = g[:, yhi * TB : (yhi + 1) * TB]
        return carry

    for place in range(4):
        z = at_of(tab, 2, place)
        inv_z = jnp.concatenate(
            [
                jnp.sum(jnp.where(line == z * 2 + yhi, inv, 0.0), axis=0, keepdims=True)
                for yhi in range(2)
            ],
            axis=1,
        )
        incoming[place].wait()
        for h in range(2):
            row0 = lax.broadcasted_iota(jnp.int32, (rows, 2 * TB), 0) + tab[24 + h]
            lax.fori_loop(
                0,
                VB // rows,
                functools.partial(
                    chunk, place=place, h=h, inv_z=inv_z, rinv=rinv_ref[z],
                    bend=bend_ref[place], tgt=tgt_ref[z], row0=row0,
                ),
                0,
            )
    for copy in outgoing[:4]:
        copy.start()
    pieces(
        tab, 1, gz, gy, weights, away,
        lambda p: incoming[4 + p].wait(), lambda p: outgoing[4 + p].start(),
    )
    for copy in outgoing:
        copy.wait()


def keep_kernel(tab, gz_ref, gy_ref, *refs):
    w_refs, out_refs = refs[:3], refs[3:6]
    gz, w0, w1, gy, w2, kept0, kept1, kept2, in_sems, out_sems = refs[6:]
    kept = (kept0, kept1, kept2)
    incoming = copies(
        [(gz_ref, gz), (w_refs[0], w0), (w_refs[1], w1), (gy_ref, gy), (w_refs[2], w2)], in_sems
    )
    outgoing = copies(list(zip(kept, out_refs)), out_sems)
    for copy in incoming:
        copy.start()

    def ready(p):
        for copy in ((0, 1), (2,), (3, 4))[p]:
            incoming[copy].wait()

    pieces(tab, 0, gz, gy, (w0, w1, w2), kept, ready, lambda p: outgoing[p].start())
    for copy in outgoing:
        copy.wait()


HALF = (32, PT, TB)
GZ = (4, 2 * VB, 2 * TB)
GR = (4, VB, 2 * TB)
GY = (2, 2, 2 * VB, 2 * TB)
W_SHAPES = ((2, 4, PT, 2 * VB), (4, 2, PT, 2 * VB), (2, 4, PT, 2 * VB))


def bf16_out(*shapes):
    return [jax.ShapeDtypeStruct(shape, BF) for shape in shapes]


def bf16_vmem(*shapes):
    return [pltpu.VMEM(shape, BF) for shape in shapes]


def grad_call(tab, expo, bend, totals, rinv, tgt, turned):
    return pl.pallas_call(
        grad_kernel,
        in_specs=[SMEM_SPEC, ANYWHERE] + [VMEM_SPEC] * 4 + [ANYWHERE] * 3,
        out_specs=[ANYWHERE] * 7,
        out_shape=bf16_out(GR, GR, GZ, GY, HALF, HALF, HALF),
        scratch_shapes=[pltpu.VMEM(GZ, F32)]
        + bf16_vmem(*W_SHAPES, GZ, GZ, GY, HALF, HALF, HALF)
        + [pltpu.SemaphoreType.DMA((7,)), pltpu.SemaphoreType.DMA((7,))],
        compiler_params=pltpu.CompilerParams(vmem_limit_bytes=VMEM),
        cost_estimate=pl.CostEstimate(
            flops=1024 * 1024 * D, bytes_accessed=24_000_000, transcendentals=0
        ),
        name="grad",
    )(tab, expo, bend, totals, rinv, tgt, *turned)


def keep_call(tab, gz, gy, turned):
    return pl.pallas_call(
        keep_kernel,
        in_specs=[SMEM_SPEC] + [ANYWHERE] * 5,
        out_specs=[ANYWHERE] * 3,
        out_shape=bf16_out(HALF, HALF, HALF),
        scratch_shapes=bf16_vmem(
            GZ, W_SHAPES[0], W_SHAPES[1], GY, W_SHAPES[2], HALF, HALF, HALF
        )
        + [pltpu.SemaphoreType.DMA((5,)), pltpu.SemaphoreType.DMA((3,))],
        compiler_params=pltpu.CompilerParams(vmem_limit_bytes=VMEM),
        cost_estimate=pl.CostEstimate(
            flops=1024 * D, bytes_accessed=1_000_000, transcendentals=0
        ),
        name="keep",
    )(tab, gz, gy, *turned)


def head_kernel(own_gr, twin_gr, own_xt, twin_xt, w, *refs):
    head_ref, gain_ref = refs[-2:]
    got = lax.dot_general(
        jnp.concatenate([gr[z] for gr in (own_gr, twin_gr) for z in range(4)], axis=1),
        jnp.concatenate([xt[z] for xt in (own_xt, twin_xt) for z in range(4)], axis=1),
        (((1,), (1,)), ((), ())), preferred_element_type=F32,
    )
    head_ref[...] = got.astype(BF)
    gain = jnp.sum(got * w[...].astype(F32), axis=0, keepdims=True)
    for i in range(gain_ref.shape[1]):
        gain_ref[0, i : i + 1, :] = gain[:, i * TB : (i + 1) * TB]


TILE = 768


def head_call(grs, xts, w, first, count, held=()):
    cols = pl.BlockSpec((VB, TILE), lambda f: (0, f + first))
    rows = pl.BlockSpec(GR, lambda f: (0, 0, 0), pipeline_mode=pl.Buffered(1))
    tokens = pl.BlockSpec((4, TILE, 2 * TB), lambda f: (0, f + first, 0))
    return pl.pallas_call(
        head_kernel,
        grid=(count,),
        in_specs=[rows, rows, tokens, tokens, cols] + [ANYWHERE] * len(held),
        out_specs=[cols, pl.BlockSpec((1, TILE // TB, TB), lambda f: (f, 0, 0))],
        out_shape=bf16_out((VB, D)) + [jax.ShapeDtypeStruct((count, TILE // TB, TB), F32)],
        input_output_aliases={5 + i: i for i in range(len(held))},
        compiler_params=pltpu.CompilerParams(vmem_limit_bytes=VMEM),
        cost_estimate=pl.CostEstimate(
            flops=1024 * D, bytes_accessed=1_000_000, transcendentals=0
        ),
        name="head",
    )(*grs, *xts, w, *held)


def sum_kernel(terms, *refs):
    ins, outs = refs[: 3 * terms], refs[3 * terms :]
    for p in range(3):
        blocks = [a[...] for a in ins[terms * p : terms * (p + 1)]]
        got = functools.reduce(lambda a, b: a + b, blocks)
        if len(outs) == 3:
            outs[p][...] = got
        else:
            outs[-1][:, p * PT : (p + 1) * PT, :] = got
    if len(outs) == 2:
        outs[-1][:, FB : FB + SQ, :] = outs[0][...]


def sum_call(here, count, gains=None):
    step = count // 2
    terms = len(here[0])
    specs = [
        pl.BlockSpec((step, PT, TB), lambda i, first=first // step: (i + first, 0, 0))
        for part in here
        for _, first in part
    ]
    arrays = [a for part in here for a, _ in part]
    if gains is None:
        out_specs = [pl.BlockSpec((step, PT, TB), lambda i: (i, 0, 0))] * 3
        out_shape = bf16_out(*[(count, PT, TB)] * 3)
    else:
        specs.append(pl.BlockSpec((step, SQ, TB), lambda i: (i, 0, 0)))
        arrays.append(gains)
        out_specs = pl.BlockSpec((step, FB + SQ, TB), lambda i: (i, 0, 0))
        out_shape = bf16_out((count, FB + SQ, TB))[0]
    return pl.pallas_call(
        functools.partial(sum_kernel, terms),
        grid=(count // step,),
        in_specs=specs,
        out_specs=out_specs,
        out_shape=out_shape,
        compiler_params=pltpu.CompilerParams(vmem_limit_bytes=VMEM),
        cost_estimate=pl.CostEstimate(flops=4 << 20, bytes_accessed=6_000_000, transcendentals=0),
        name="sum%d" % terms,
    )(*arrays)


def shards(section_output, norm_gain, head_weight, targets):
    x, ylo, yhi, z, core = (lax.axis_index(a) for a in AX)
    y = yhi * 2 + ylo
    shard = (((x * 2 + ylo) * 2 + yhi) * 4 + z) * 2 + core
    tab = table(x, y, z, core, shard)

    xt = section_output.T.astype(F32)
    gain = norm_gain.astype(F32)[:, None]
    scaled_x = (xt * gain).astype(BF)
    squares = jnp.sum(xt * xt, axis=0, keepdims=True)
    extra = jnp.concatenate(
        split3(squares) + [jnp.zeros((SQ - 3, TB), BF)], axis=0
    )
    block = jnp.concatenate([scaled_x[:PT], extra, scaled_x[PT:]], axis=0)
    other = send(head_weight, TWIN)
    turned = flip(head_weight, other)

    tgt = lax.dynamic_index_in_dim(
        targets.reshape(2, 4, 2, TB), core, axis=2, keepdims=False
    ).transpose(1, 0, 2).reshape(4, 1, 2 * TB)
    halves = gather(block)
    owner = jnp.stack([tab[ex] * 2 + (tab[4 + ey] & 1) for ex, ey, _ in BITS])
    owner = (owner[:, None, None] == jnp.arange(8, dtype=jnp.int32)[None, :, None]).astype(F32)
    halves, turned, tgt, tab, owner = lax.optimization_barrier((halves, turned, tgt, tab, owner))

    expo, bend, rinv, stats, xt_all = act_call(tab, halves, head_weight, other, tgt)
    stats = lax.all_to_all(stats, AX[:4], 0, 0)
    stats, xt_all = lax.optimization_barrier((stats, xt_all))
    xts = (xt_all, send(xt_all, TWIN))

    own_gr, other_gr, gz, gy, *away = grad_call(tab, expo, bend, stats, rinv, tgt, turned)

    bound = lax.optimization_barrier

    def exchange(away, phase):
        return [send(away[p], across(ORDER[p][phase])) for p in range(3)]

    got1 = exchange(away, 2)
    grs = (own_gr, send(other_gr, TWIN))
    kept = keep_call(tab, gz, gy, turned)
    kept, grs = bound((kept, grs))
    head_grad, gain0 = head_call(grs, xts, head_weight, 0, 4)
    got1, kept, grs, head_grad, gain0 = bound((got1, kept, grs, head_grad, gain0))
    away = sum_call([[(kept[p], 16), (got1[p], 16)] for p in range(3)], 16)

    away, grs, head_grad = bound((away, grs, head_grad))
    got2 = exchange(away, 1)
    head_grad, gain1 = head_call(grs, xts, head_weight, 4, 2, (head_grad,))
    gains = jnp.concatenate([gain0, gain1])
    gains = gains + send(gains, across(1))
    got2, gains = bound((got2, gains))
    more = send(gains, across(0))
    away = sum_call([[(kept[p], 8), (got1[p], 8), (got2[p], 8)] for p in range(3)], 8)

    away, more, gains = bound((away, more, gains))
    got3 = exchange(away, 0)
    gains = gains + more
    more = send(gains, across(2))
    got3, more = bound((got3, more))
    gains = gains + more
    here = [[(a[p], 0) for a in (kept, got1, got2, got3)] for p in range(3)]

    gains = jnp.sum(owner * gains.reshape(1, 8, FB), axis=1)
    gains = jnp.concatenate([gains, jnp.zeros((8, 5 * TB - FB), F32)], axis=1)
    gains = jnp.stack(split3(gains) + [jnp.zeros((8, 5 * TB), BF)], axis=1)
    gains = gains.reshape(8, 20, TB)[:, :SQ]

    blocks = in_cube(sum_call(here, 8, gains))
    blocks = jnp.sum(blocks.astype(F32), axis=0)
    grad_hidden = blocks[:FB]
    gains = jnp.sum(blocks[FB : FB + 15].reshape(3, 5 * TB), axis=0)[:FB]
    gain_grad = (gains + send(gains, TWIN)) / norm_gain.astype(F32)

    row = jnp.sum(stats, axis=0)
    picked, slope, slope_at = row[8:9], row[9:10], row[10:11]
    sum_exp = lax.dynamic_slice(row, (z * 2 + yhi, 0), (1, TB))
    rinv = lax.dynamic_slice(rinv, (z, 0, yhi * TB), (1, 1, TB)).reshape(1, TB)
    token_loss = (jnp.log(sum_exp) - picked).reshape(TB)
    inner = slope / sum_exp - slope_at
    grad_input = (rinv * (grad_hidden * gain) - xt * (rinv * rinv * inner / D)).astype(BF).T
    return (token_loss, grad_input, head_grad, gain_grad)


def solution(mesh):
    fine = Mesh(mesh.devices.reshape(4, 2, 2, 4, 2), AX)
    pipe, dp = ("x", "ylo"), ("yhi", "z", "core")
    return jax.shard_map(
        shards,
        mesh=fine,
        in_specs=(P(dp, pipe), P(pipe), P(pipe + dp, None), P()),
        out_specs=(P(dp), P(dp, pipe), P(pipe + dp, None), P(pipe)),
        check_vma=False,
    )
```

```python
import functools
import itertools

import jax
import jax.numpy as jnp
import numpy as np
from jax import lax
from jax.experimental import pallas as pl
from jax.experimental.pallas import tpu as pltpu
from jax.sharding import Mesh, PartitionSpec as P

AX = ("x", "ylo", "yhi", "z", "core")
D = 4608
FB = 576
PT = 192
SQ = 16
TB = 128
VB = 512
CAP = 30.0
EPS = 1e-06
VMEM = 60 * 1024 * 1024
BF = jnp.bfloat16
F32 = jnp.float32

ORDER = ((0, 1, 2), (1, 2, 0), (2, 0, 1))


def coords(i):
    core, z, yhi, ylo, x = i % 2, i // 2 % 4, i // 8 % 2, i // 16 % 2, i // 32
    return [x, yhi * 2 + ylo, z], core


def number(c, core):
    return (((c[0] * 2 + c[1] % 2) * 2 + c[1] // 2) * 4 + c[2]) * 2 + core


def from_bits(core, late, early):
    gray = late * 2 + early if core == 0 else early * 2 + late
    return gray ^ (gray >> 1)


BITS = list(itertools.product((0, 1), repeat=3))
CUBES = [
    [number([from_bits(core, b, e) for b, e in zip(late, early)], core) for early in BITS]
    for core in (0, 1)
    for late in BITS
]
TWIN = [(i, i ^ 1) for i in range(128)]


@functools.cache
def across(dim):
    pairs = []
    for i in range(128):
        c, core = coords(i)
        gray = (c[dim] ^ (c[dim] >> 1)) ^ (2 if core == 0 else 1)
        c[dim] = gray ^ (gray >> 1)
        pairs.append((i, number(c, core)))
    return pairs


def send(a, pairs):
    return lax.ppermute(a, AX, pairs)


def in_cube(a):
    return lax.all_to_all(a, AX, 0, 0, axis_index_groups=CUBES)


def gather(block):
    cube = in_cube(jnp.broadcast_to(block[None], (8,) + block.shape))
    cuts = (0, PT + SQ, 2 * PT + SQ, 3 * PT + SQ)
    held = [cube[:, cuts[p] : cuts[p + 1]] for p in range(3)]
    for phase in range(2):
        got = [send(held[p], across(ORDER[p][phase])) for p in range(3)]
        held = [jnp.concatenate([held[p], got[p]]) for p in range(3)]
    got = [send(held[p], across(ORDER[p][2])) for p in range(3)]
    return [a for p in range(3) for a in (held[p], got[p])]


def block_at(part, places):
    late = [place >> 1 for place in places]
    early = [place & 1 for place in places]
    first, second, _ = ORDER[part]
    return (late[second] * 2 + late[first]) * 8 + early[0] * 4 + early[1] * 2 + early[2]


def split3(v):
    hi = lax.reduce_precision(v, 8, 7)
    mid = lax.reduce_precision(v - hi, 8, 7)
    lo = v - hi - mid
    return [hi.astype(BF), mid.astype(BF), lo.astype(BF)]


def table(x, y, z, core, shard):
    out = []
    place = jnp.arange(4, dtype=jnp.int32)

    def swap(bits):
        return jnp.where(core == 0, bits, (bits & 1) * 2 + (bits >> 1))

    mine = [swap(c ^ (c >> 1)) & 2 for c in (x, y, z)]
    for late in mine:
        gray = swap(place ^ late)
        out.append(gray ^ (gray >> 1))
    for late in mine:
        out.append(swap(place ^ (place >> 1)) ^ late)
    out.append(jnp.stack([shard * VB, (shard ^ 1) * VB]))
    return jnp.concatenate(out).astype(jnp.int32)


def at_of(tab, dim, place):
    return tab[4 * dim + place]


def place_of(tab, dim, at):
    return tab[12 + 4 * dim + at]


def flip_kernel(own_ref, other_ref, a_ref, b_ref, c_ref):
    for h, ref in enumerate((own_ref, other_ref)):
        turned = ref[...].T
        cols = pl.ds(h * VB, VB)
        for ylo in range(2):
            at = ylo * FB
            a_ref[ylo, 0, :, cols] = turned[at : at + PT]
            b_ref[0, ylo, :, cols] = turned[at + PT : at + 2 * PT]
            c_ref[ylo, 0, :, cols] = turned[at + 2 * PT : at + 3 * PT]


def flip(own, other):
    block = pl.BlockSpec((VB, 2 * FB), lambda x: (0, x))
    return pl.pallas_call(
        flip_kernel,
        grid=(4,),
        in_specs=[block, block],
        out_specs=[
            pl.BlockSpec((2, 1, PT, 2 * VB), lambda x: (0, x, 0, 0)),
            pl.BlockSpec((1, 2, PT, 2 * VB), lambda x: (x, 0, 0, 0)),
            pl.BlockSpec((2, 1, PT, 2 * VB), lambda x: (0, x, 0, 0)),
        ],
        out_shape=[
            jax.ShapeDtypeStruct((2, 4, PT, 2 * VB), BF),
            jax.ShapeDtypeStruct((4, 2, PT, 2 * VB), BF),
            jax.ShapeDtypeStruct((2, 4, PT, 2 * VB), BF),
        ],
        compiler_params=pltpu.CompilerParams(vmem_limit_bytes=VMEM),
        cost_estimate=pl.CostEstimate(
            flops=0, bytes_accessed=4 * VB * D * 2, transcendentals=0
        ),
        name="flip",
    )(own, other)


def act_kernel(tab, *refs):
    halves = [refs[2 * p : 2 * p + 2] for p in range(3)]
    own_ref, other_ref, tgt_ref = refs[6:9]
    expo_ref, bend_ref, rinv_ref, stat_ref, xt_out = refs[9:14]
    xt, squares, weights, acc, totals, stats, sems, out_sems, w_sems = refs[14:]
    step = pl.program_id(0)

    def fetch(src, tile, x, y, part):
        row = (x * 2 + (y & 1)) * FB + part * PT
        lanes = pl.ds(pl.multiple_of((y >> 1) * TB, TB), TB)
        pltpu.make_async_copy(
            src.at[pl.ds(0, PT)],
            xt.at[tile, pl.ds(pl.multiple_of(row, 16), PT), lanes],
            sems.at[tile],
        ).start()
        if part == 0:
            row = (x * 2 + (y & 1)) * SQ
            pltpu.make_async_copy(
                src.at[pl.ds(PT, SQ)],
                squares.at[tile, pl.ds(pl.multiple_of(row, 16), SQ), lanes],
                sems.at[tile],
            ).start()

    def issue(tile):
        for px in range(4):
            for py in range(4):
                x, y = at_of(tab, 0, px), at_of(tab, 1, py)
                places = (px, py, tile)
                fetch(halves[1][px >> 1].at[block_at(1, places)], tile, x, y, 1)
                fetch(halves[2][py >> 1].at[block_at(2, places)], tile, x, y, 2)
        for half in range(2):
            @pl.when((tile >> 1) == half)
            def _():
                for px in range(4):
                    for py in range(4):
                        fetch(
                            halves[0][half].at[block_at(0, (px, py, tile))],
                            tile, at_of(tab, 0, px), at_of(tab, 1, py), 0,
                        )

    def load(h, ref):
        return pltpu.make_async_copy(ref, weights.at[pl.ds(h * VB, VB)], w_sems.at[h])

    def arrived():
        pltpu.make_async_copy(xt.at[step], xt.at[step], sems.at[step]).wait()
        pltpu.make_async_copy(squares.at[step], squares.at[step], sems.at[step]).wait()
        pltpu.make_async_copy(xt.at[step], xt_out.at[step], out_sems.at[step]).start()

    @pl.when(step == 0)
    def _():
        load(0, own_ref).start()
        issue(step)
        load(1, other_ref).start()
        issue(step + 1)
        arrived()
        for h, ref in enumerate((own_ref, other_ref)):
            load(h, ref).wait()
            rows = pl.ds(h * VB, VB)
            acc[rows, :] = jnp.dot(weights[rows, :], xt[step], preferred_element_type=F32)

    @pl.when(step > 0)
    def _():
        @pl.when(step < 3)
        def _():
            issue(step + 1)

        arrived()
        acc[...] = jnp.dot(weights[...], xt[step], preferred_element_type=F32)

    mean = jnp.sum(squares[step].astype(F32), axis=0, keepdims=True) / D
    rinv = lax.rsqrt(mean + EPS)
    z = at_of(tab, 2, step)
    rinv_ref[z] = rinv
    tgt = tgt_ref[z]
    rows = 64
    zeros = jnp.zeros((8, 2 * TB), F32)
    sums = (zeros,) * 3
    inside = jnp.zeros((1, 2 * TB), jnp.bool_)

    def fold(v):
        return jnp.sum(v.reshape(rows // 8, 8, 2 * TB), axis=0)

    for h in range(2):
        row0 = lax.broadcasted_iota(jnp.int32, (rows, 2 * TB), 0) + tab[24 + h]
        inside = inside | ((tgt >= tab[24 + h]) & (tgt < tab[24 + h] + VB))

        def chunk(i, sums, h=h, row0=row0):
            total, slope, act_at = sums
            at = pl.multiple_of(i * rows, rows)
            here = pl.ds(h * VB + at, rows)
            act = acc[here, :] * rinv
            t = jnp.tanh(act * (1.0 / CAP))
            expo = jnp.exp(t * CAP)
            sharp = expo * (1.0 - t * t)
            expo_ref[0, here, :] = sharp
            return (
                total + fold(expo),
                slope + fold(sharp * act),
                act_at + fold(jnp.where(row0 + at == tgt, act, 0.0)),
            )

        sums = lax.fori_loop(0, VB // rows, chunk, sums)
    total, slope, act_at = [jnp.sum(s, axis=0, keepdims=True) for s in sums]
    t = jnp.tanh(act_at * (1.0 / CAP))
    bend = jnp.where(inside, 1.0 - t * t, 0.0)
    bend_ref[0] = bend
    sums = (total, t * CAP, slope, bend * act_at)
    for yhi in range(2):
        lanes = slice(yhi * TB, (yhi + 1) * TB)
        totals[pl.ds(z * 2 + yhi, 1), :] = sums[0][:, lanes]
        stats[yhi * 4 + z] = jnp.concatenate(
            [s[:, lanes] for s in sums[1:4]] + [jnp.zeros((5, TB), F32)], axis=0
        )

    @pl.when(step == 3)
    def _():
        for chip in range(64):
            stat_ref[chip, 0:8, :] = totals[...]
            stat_ref[chip, 8:16, :] = stats[chip % 8]
        for tile in range(4):
            pltpu.make_async_copy(xt.at[tile], xt_out.at[tile], out_sems.at[tile]).wait()


ANYWHERE = pl.BlockSpec(memory_space=pl.ANY)
SMEM_SPEC = pl.BlockSpec(memory_space=pltpu.SMEM)
VMEM_SPEC = pl.BlockSpec(memory_space=pltpu.VMEM)


def act_call(tab, halves, own, other, tgt):
    tile = pl.BlockSpec((1, 2 * VB, 2 * TB), lambda z, w: (z, 0, 0))
    rows = pl.BlockSpec((4, 1, 2 * TB), lambda z, w: (0, 0, 0))
    return pl.pallas_call(
        act_kernel,
        grid_spec=pltpu.PrefetchScalarGridSpec(
            num_scalar_prefetch=1,
            grid=(4,),
            in_specs=[ANYWHERE] * 8 + [rows],
            out_specs=[
                tile,
                pl.BlockSpec((1, 1, 2 * TB), lambda z, w: (z, 0, 0)),
                rows,
                pl.BlockSpec((64, 16, TB), lambda z, w: (0, 0, 0)),
                ANYWHERE,
            ],
            scratch_shapes=[
                pltpu.VMEM((4, D, 2 * TB), BF),
                pltpu.VMEM((4, 8 * SQ, 2 * TB), BF),
                pltpu.VMEM((2 * VB, D), BF),
                pltpu.VMEM((2 * VB, 2 * TB), F32),
                pltpu.VMEM((8, TB), F32),
                pltpu.VMEM((8, 8, TB), F32),
                pltpu.SemaphoreType.DMA((4,)),
                pltpu.SemaphoreType.DMA((4,)),
                pltpu.SemaphoreType.DMA((2,)),
            ],
        ),
        out_shape=[
            jax.ShapeDtypeStruct((4, 2 * VB, 2 * TB), F32),
            jax.ShapeDtypeStruct((4, 1, 2 * TB), F32),
            jax.ShapeDtypeStruct((4, 1, 2 * TB), F32),
            jax.ShapeDtypeStruct((64, 16, TB), F32),
            jax.ShapeDtypeStruct((4, D, 2 * TB), BF),
        ],
        compiler_params=pltpu.CompilerParams(vmem_limit_bytes=VMEM),
        cost_estimate=pl.CostEstimate(
            flops=2 * 1024 * 1024 * D, bytes_accessed=30_000_000, transcendentals=2 << 20
        ),
        name="act",
    )(tab, *halves, own, other, tgt)


def pieces(tab, lead, gz, gy, weights, outs, ready, done):
    w0, w1, w2 = weights
    out0, out1, out2 = outs
    ready(0)
    w = w0[...].reshape(8 * PT, 2 * VB)
    both = jnp.concatenate([gz[lead * 2], gz[lead * 2 + 1]], axis=1)
    got = jnp.dot(w, both, preferred_element_type=F32).astype(BF)
    for low in range(2):
        for x in range(4):
            for ylo in range(2):
                for yhi in range(2):
                    places = (place_of(tab, 0, x), place_of(tab, 1, yhi * 2 + ylo), lead * 2 + low)
                    row, lane = (ylo * 4 + x) * PT, (low * 2 + yhi) * TB
                    out0[block_at(0, places)] = got[row : row + PT, lane : lane + TB]
    done(0)
    ready(1)
    for low in range(2):
        place = lead * 2 + low
        x = at_of(tab, 0, place)
        w = w1[x].reshape(2 * PT, 2 * VB)
        tokens = jnp.concatenate([gz[z] for z in range(4)], axis=1)
        got = jnp.dot(w, tokens, preferred_element_type=F32).astype(BF)
        for z in range(4):
            for ylo in range(2):
                for yhi in range(2):
                    places = (place, place_of(tab, 1, yhi * 2 + ylo), z)
                    row, lane = ylo * PT, (z * 2 + yhi) * TB
                    out1[block_at(1, places)] = got[row : row + PT, lane : lane + TB]
    done(1)
    ready(2)
    for low in range(2):
        place = lead * 2 + low
        y = at_of(tab, 1, place)
        w = w2[y & 1].reshape(4 * PT, 2 * VB)
        tokens = jnp.concatenate([gy[y >> 1, pair] for pair in range(2)], axis=1)
        got = jnp.dot(w, tokens, preferred_element_type=F32).astype(BF)
        for x in range(4):
            for z in range(4):
                places = (place_of(tab, 0, x), place, z)
                out2[block_at(2, places)] = got[x * PT : (x + 1) * PT, z * TB : (z + 1) * TB]
    done(2)


def copies(pairs, sems):
    return [
        pltpu.make_async_copy(src, dst, sems.at[i]) for i, (src, dst) in enumerate(pairs)
    ]


def grad_kernel(tab, expo_ref, bend_ref, totals_ref, rinv_ref, tgt_ref, *refs):
    w_refs, out_refs = refs[:3], refs[3:10]
    expo, w0, w1, w2, gz, gr, gy, away0, away1, away2, in_sems, out_sems = refs[10:]
    weights, away = (w0, w1, w2), (away0, away1, away2)
    tiles = [(expo_ref.at[i], expo.at[i]) for i in range(4)]
    incoming = copies(tiles + list(zip(w_refs, weights)), in_sems)
    by_rows = (gr.at[:, pl.ds(0, VB)], gr.at[:, pl.ds(VB, VB)])
    outgoing = copies(list(zip(by_rows + (gz, gy) + away, out_refs)), out_sems)
    for copy in incoming:
        copy.start()
    rows = 64
    inv = 1.0 / jnp.sum(totals_ref[...], axis=0)[0:8]
    line = lax.broadcasted_iota(jnp.int32, (8, TB), 0)

    def chunk(i, carry, place, h, inv_z, rinv, bend, tgt, row0):
        at = pl.multiple_of(i * rows, rows)
        here = pl.ds(h * VB + at, rows)
        g = expo[place, here, :] * inv_z - jnp.where(row0 + at == tgt, bend, 0.0)
        gr[place, here, :] = (g * rinv).astype(BF)
        g = g.astype(BF)
        gz[place, here, :] = g
        for yhi in range(2):
            gy[yhi, place // 2, here, pl.ds(place % 2 * TB, TB)] = g[:, yhi * TB : (yhi + 1) * TB]
        return carry

    for place in range(4):
        z = at_of(tab, 2, place)
        inv_z = jnp.concatenate(
            [
                jnp.sum(jnp.where(line == z * 2 + yhi, inv, 0.0), axis=0, keepdims=True)
                for yhi in range(2)
            ],
            axis=1,
        )
        incoming[place].wait()
        for h in range(2):
            row0 = lax.broadcasted_iota(jnp.int32, (rows, 2 * TB), 0) + tab[24 + h]
            lax.fori_loop(
                0,
                VB // rows,
                functools.partial(
                    chunk, place=place, h=h, inv_z=inv_z, rinv=rinv_ref[z],
                    bend=bend_ref[place], tgt=tgt_ref[z], row0=row0,
                ),
                0,
            )
    for copy in outgoing[:4]:
        copy.start()
    pieces(
        tab, 1, gz, gy, weights, away,
        lambda p: incoming[4 + p].wait(), lambda p: outgoing[4 + p].start(),
    )
    for copy in outgoing:
        copy.wait()


def keep_kernel(tab, gz_ref, gy_ref, *refs):
    w_refs, out_refs = refs[:3], refs[3:6]
    gz, w0, w1, gy, w2, kept0, kept1, kept2, in_sems, out_sems = refs[6:]
    kept = (kept0, kept1, kept2)
    incoming = copies(
        [(gz_ref, gz), (w_refs[0], w0), (w_refs[1], w1), (gy_ref, gy), (w_refs[2], w2)], in_sems
    )
    outgoing = copies(list(zip(kept, out_refs)), out_sems)
    for copy in incoming:
        copy.start()

    def ready(p):
        for copy in ((0, 1), (2,), (3, 4))[p]:
            incoming[copy].wait()

    pieces(tab, 0, gz, gy, (w0, w1, w2), kept, ready, lambda p: outgoing[p].start())
    for copy in outgoing:
        copy.wait()


HALF = (32, PT, TB)
GZ = (4, 2 * VB, 2 * TB)
GR = (4, VB, 2 * TB)
GY = (2, 2, 2 * VB, 2 * TB)
W_SHAPES = ((2, 4, PT, 2 * VB), (4, 2, PT, 2 * VB), (2, 4, PT, 2 * VB))


def bf16_out(*shapes):
    return [jax.ShapeDtypeStruct(shape, BF) for shape in shapes]


def bf16_vmem(*shapes):
    return [pltpu.VMEM(shape, BF) for shape in shapes]


def grad_call(tab, expo, bend, totals, rinv, tgt, turned):
    return pl.pallas_call(
        grad_kernel,
        in_specs=[SMEM_SPEC, ANYWHERE] + [VMEM_SPEC] * 4 + [ANYWHERE] * 3,
        out_specs=[ANYWHERE] * 7,
        out_shape=bf16_out(GR, GR, GZ, GY, HALF, HALF, HALF),
        scratch_shapes=[pltpu.VMEM(GZ, F32)]
        + bf16_vmem(*W_SHAPES, GZ, GZ, GY, HALF, HALF, HALF)
        + [pltpu.SemaphoreType.DMA((7,)), pltpu.SemaphoreType.DMA((7,))],
        compiler_params=pltpu.CompilerParams(vmem_limit_bytes=VMEM),
        cost_estimate=pl.CostEstimate(
            flops=1024 * 1024 * D, bytes_accessed=24_000_000, transcendentals=0
        ),
        name="grad",
    )(tab, expo, bend, totals, rinv, tgt, *turned)


def keep_call(tab, gz, gy, turned):
    return pl.pallas_call(
        keep_kernel,
        in_specs=[SMEM_SPEC] + [ANYWHERE] * 5,
        out_specs=[ANYWHERE] * 3,
        out_shape=bf16_out(HALF, HALF, HALF),
        scratch_shapes=bf16_vmem(
            GZ, W_SHAPES[0], W_SHAPES[1], GY, W_SHAPES[2], HALF, HALF, HALF
        )
        + [pltpu.SemaphoreType.DMA((5,)), pltpu.SemaphoreType.DMA((3,))],
        compiler_params=pltpu.CompilerParams(vmem_limit_bytes=VMEM),
        cost_estimate=pl.CostEstimate(
            flops=1024 * D, bytes_accessed=1_000_000, transcendentals=0
        ),
        name="keep",
    )(tab, gz, gy, *turned)


def head_kernel(own_gr, twin_gr, own_xt, twin_xt, w, *refs):
    head_ref, gain_ref = refs[-2:]
    got = lax.dot_general(
        jnp.concatenate([gr[z] for gr in (own_gr, twin_gr) for z in range(4)], axis=1),
        jnp.concatenate([xt[z] for xt in (own_xt, twin_xt) for z in range(4)], axis=1),
        (((1,), (1,)), ((), ())), preferred_element_type=F32,
    )
    head_ref[...] = got.astype(BF)
    gain = jnp.sum(got * w[...].astype(F32), axis=0, keepdims=True)
    for i in range(gain_ref.shape[1]):
        gain_ref[0, i : i + 1, :] = gain[:, i * TB : (i + 1) * TB]


TILE = 768


def head_call(grs, xts, w, first, count, held=()):
    cols = pl.BlockSpec((VB, TILE), lambda f: (0, f + first))
    rows = pl.BlockSpec(GR, lambda f: (0, 0, 0), pipeline_mode=pl.Buffered(1))
    tokens = pl.BlockSpec((4, TILE, 2 * TB), lambda f: (0, f + first, 0))
    return pl.pallas_call(
        head_kernel,
        grid=(count,),
        in_specs=[rows, rows, tokens, tokens, cols] + [ANYWHERE] * len(held),
        out_specs=[cols, pl.BlockSpec((1, TILE // TB, TB), lambda f: (f, 0, 0))],
        out_shape=bf16_out((VB, D)) + [jax.ShapeDtypeStruct((count, TILE // TB, TB), F32)],
        input_output_aliases={5 + i: i for i in range(len(held))},
        compiler_params=pltpu.CompilerParams(vmem_limit_bytes=VMEM),
        cost_estimate=pl.CostEstimate(
            flops=1024 * D, bytes_accessed=1_000_000, transcendentals=0
        ),
        name="head",
    )(*grs, *xts, w, *held)


def sum_kernel(terms, *refs):
    ins, outs = refs[: 3 * terms], refs[3 * terms :]
    for p in range(3):
        blocks = [a[...] for a in ins[terms * p : terms * (p + 1)]]
        got = functools.reduce(lambda a, b: a + b, blocks)
        if len(outs) == 3:
            outs[p][...] = got
        else:
            outs[-1][:, p * PT : (p + 1) * PT, :] = got
    if len(outs) == 2:
        outs[-1][:, FB : FB + SQ, :] = outs[0][...]


def sum_call(here, count, gains=None):
    step = count // 2
    terms = len(here[0])
    specs = [
        pl.BlockSpec((step, PT, TB), lambda i, first=first // step: (i + first, 0, 0))
        for part in here
        for _, first in part
    ]
    arrays = [a for part in here for a, _ in part]
    if gains is None:
        out_specs = [pl.BlockSpec((step, PT, TB), lambda i: (i, 0, 0))] * 3
        out_shape = bf16_out(*[(count, PT, TB)] * 3)
    else:
        specs.append(pl.BlockSpec((step, SQ, TB), lambda i: (i, 0, 0)))
        arrays.append(gains)
        out_specs = pl.BlockSpec((step, FB + SQ, TB), lambda i: (i, 0, 0))
        out_shape = bf16_out((count, FB + SQ, TB))[0]
    return pl.pallas_call(
        functools.partial(sum_kernel, terms),
        grid=(count // step,),
        in_specs=specs,
        out_specs=out_specs,
        out_shape=out_shape,
        compiler_params=pltpu.CompilerParams(vmem_limit_bytes=VMEM),
        cost_estimate=pl.CostEstimate(flops=4 << 20, bytes_accessed=6_000_000, transcendentals=0),
        name="sum%d" % terms,
    )(*arrays)


def shards(section_output, norm_gain, head_weight, targets):
    x, ylo, yhi, z, core = (lax.axis_index(a) for a in AX)
    y = yhi * 2 + ylo
    shard = (((x * 2 + ylo) * 2 + yhi) * 4 + z) * 2 + core
    tab = table(x, y, z, core, shard)

    xt = section_output.T.astype(F32)
    gain = norm_gain.astype(F32)[:, None]
    scaled_x = (xt * gain).astype(BF)
    squares = jnp.sum(xt * xt, axis=0, keepdims=True)
    extra = jnp.concatenate(
        split3(squares) + [jnp.zeros((SQ - 3, TB), BF)], axis=0
    )
    block = jnp.concatenate([scaled_x[:PT], extra, scaled_x[PT:]], axis=0)
    other = send(head_weight, TWIN)
    turned = flip(head_weight, other)

    tgt = lax.dynamic_index_in_dim(
        targets.reshape(2, 4, 2, TB), core, axis=2, keepdims=False
    ).transpose(1, 0, 2).reshape(4, 1, 2 * TB)
    halves = gather(block)
    owner = jnp.stack([tab[ex] * 2 + (tab[4 + ey] & 1) for ex, ey, _ in BITS])
    owner = (owner[:, None, None] == jnp.arange(8, dtype=jnp.int32)[None, :, None]).astype(F32)
    halves, turned, tgt, tab, owner = lax.optimization_barrier((halves, turned, tgt, tab, owner))

    expo, bend, rinv, stats, xt_all = act_call(tab, halves, head_weight, other, tgt)
    stats = lax.all_to_all(stats, AX[:4], 0, 0)
    stats, xt_all = lax.optimization_barrier((stats, xt_all))
    xts = (xt_all, send(xt_all, TWIN))

    own_gr, other_gr, gz, gy, *away = grad_call(tab, expo, bend, stats, rinv, tgt, turned)

    bound = lax.optimization_barrier

    def exchange(away, phase):
        return [send(away[p], across(ORDER[p][phase])) for p in range(3)]

    got1 = exchange(away, 2)
    grs = (own_gr, send(other_gr, TWIN))
    kept = keep_call(tab, gz, gy, turned)
    kept, grs = bound((kept, grs))
    head_grad, gain0 = head_call(grs, xts, head_weight, 0, 4)
    got1, kept, grs, head_grad, gain0 = bound((got1, kept, grs, head_grad, gain0))
    away = sum_call([[(kept[p], 16), (got1[p], 16)] for p in range(3)], 16)

    away, grs, head_grad = bound((away, grs, head_grad))
    got2 = exchange(away, 1)
    head_grad, gain1 = head_call(grs, xts, head_weight, 4, 2, (head_grad,))
    gains = jnp.concatenate([gain0, gain1])
    gains = gains + send(gains, across(1))
    got2, gains = bound((got2, gains))
    more = send(gains, across(0))
    away = sum_call([[(kept[p], 8), (got1[p], 8), (got2[p], 8)] for p in range(3)], 8)

    away, more, gains = bound((away, more, gains))
    got3 = exchange(away, 0)
    gains = gains + more
    more = send(gains, across(2))
    got3, more = bound((got3, more))
    gains = gains + more
    here = [[(a[p], 0) for a in (kept, got1, got2, got3)] for p in range(3)]

    gains = jnp.sum(owner * gains.reshape(1, 8, FB), axis=1)
    gains = jnp.concatenate([gains, jnp.zeros((8, 5 * TB - FB), F32)], axis=1)
    gains = jnp.stack(split3(gains) + [jnp.zeros((8, 5 * TB), BF)], axis=1)
    gains = gains.reshape(8, 20, TB)[:, :SQ]

    blocks = in_cube(sum_call(here, 8, gains))
    blocks = jnp.sum(blocks.astype(F32), axis=0)
    grad_hidden = blocks[:FB]
    gains = jnp.sum(blocks[FB : FB + 15].reshape(3, 5 * TB), axis=0)[:FB]
    gain_grad = (gains + send(gains, TWIN)) / norm_gain.astype(F32)

    row = jnp.sum(stats, axis=0)
    picked, slope, slope_at = row[8:9], row[9:10], row[10:11]
    sum_exp = lax.dynamic_slice(row, (z * 2 + yhi, 0), (1, TB))
    rinv = lax.dynamic_slice(rinv, (z, 0, yhi * TB), (1, 1, TB)).reshape(1, TB)
    token_loss = (jnp.log(sum_exp) - picked).reshape(TB)
    inner = slope / sum_exp - slope_at
    grad_input = (rinv * (grad_hidden * gain) - xt * (rinv * rinv * inner / D)).astype(BF).T
    return (token_loss, grad_input, head_grad, gain_grad)


def solution(mesh):
    fine = Mesh(mesh.devices.reshape(4, 2, 2, 4, 2), AX)
    pipe, dp = ("x", "ylo"), ("yhi", "z", "core")
    return jax.shard_map(
        shards,
        mesh=fine,
        in_specs=(P(dp, pipe), P(pipe), P(pipe + dp, None), P()),
        out_specs=(P(dp), P(dp, pipe), P(pipe + dp, None), P(pipe)),
        check_vma=False,
    )
```

```python
import functools
import itertools

import jax
import jax.numpy as jnp
import numpy as np
from jax import lax
from jax.experimental import pallas as pl
from jax.experimental.pallas import tpu as pltpu
from jax.sharding import Mesh, PartitionSpec as P

AX = ("x", "ylo", "yhi", "z", "core")
D = 4608
FB = 576
PT = 192
SQ = 16
TB = 128
VB = 512
CAP = 30.0
EPS = 1e-06
VMEM = 60 * 1024 * 1024
BF = jnp.bfloat16
F32 = jnp.float32

ORDER = ((0, 1, 2), (1, 2, 0), (2, 0, 1))


def coords(i):
    core, z, yhi, ylo, x = i % 2, i // 2 % 4, i // 8 % 2, i // 16 % 2, i // 32
    return [x, yhi * 2 + ylo, z], core


def number(c, core):
    return (((c[0] * 2 + c[1] % 2) * 2 + c[1] // 2) * 4 + c[2]) * 2 + core


def from_bits(core, late, early):
    gray = late * 2 + early if core == 0 else early * 2 + late
    return gray ^ (gray >> 1)


BITS = list(itertools.product((0, 1), repeat=3))
CUBES = [
    [number([from_bits(core, b, e) for b, e in zip(late, early)], core) for early in BITS]
    for core in (0, 1)
    for late in BITS
]
TWIN = [(i, i ^ 1) for i in range(128)]


@functools.cache
def across(dim):
    pairs = []
    for i in range(128):
        c, core = coords(i)
        gray = (c[dim] ^ (c[dim] >> 1)) ^ (2 if core == 0 else 1)
        c[dim] = gray ^ (gray >> 1)
        pairs.append((i, number(c, core)))
    return pairs


def send(a, pairs):
    return lax.ppermute(a, AX, pairs)


def in_cube(a):
    return lax.all_to_all(a, AX, 0, 0, axis_index_groups=CUBES)


def gather(block):
    cube = in_cube(jnp.broadcast_to(block[None], (8,) + block.shape))
    cuts = (0, PT + SQ, 2 * PT + SQ, 3 * PT + SQ)
    held = [cube[:, cuts[p] : cuts[p + 1]] for p in range(3)]
    for phase in range(2):
        got = [send(held[p], across(ORDER[p][phase])) for p in range(3)]
        held = [jnp.concatenate([held[p], got[p]]) for p in range(3)]
    got = [send(held[p], across(ORDER[p][2])) for p in range(3)]
    return [a for p in range(3) for a in (held[p], got[p])]


def block_at(part, places):
    late = [place >> 1 for place in places]
    early = [place & 1 for place in places]
    first, second, _ = ORDER[part]
    return (late[second] * 2 + late[first]) * 8 + early[0] * 4 + early[1] * 2 + early[2]


def split3(v):
    hi = lax.reduce_precision(v, 8, 7)
    mid = lax.reduce_precision(v - hi, 8, 7)
    lo = v - hi - mid
    return [hi.astype(BF), mid.astype(BF), lo.astype(BF)]


def table(x, y, z, core, shard):
    out = []
    place = jnp.arange(4, dtype=jnp.int32)

    def swap(bits):
        return jnp.where(core == 0, bits, (bits & 1) * 2 + (bits >> 1))

    mine = [swap(c ^ (c >> 1)) & 2 for c in (x, y, z)]
    for late in mine:
        gray = swap(place ^ late)
        out.append(gray ^ (gray >> 1))
    for late in mine:
        out.append(swap(place ^ (place >> 1)) ^ late)
    out.append(jnp.stack([shard * VB, (shard ^ 1) * VB]))
    return jnp.concatenate(out).astype(jnp.int32)


def at_of(tab, dim, place):
    return tab[4 * dim + place]


def place_of(tab, dim, at):
    return tab[12 + 4 * dim + at]


def flip_kernel(own_ref, other_ref, a_ref, b_ref, c_ref):
    for h, ref in enumerate((own_ref, other_ref)):
        turned = ref[...].T
        cols = pl.ds(h * VB, VB)
        for ylo in range(2):
            at = ylo * FB
            a_ref[ylo, 0, :, cols] = turned[at : at + PT]
            b_ref[0, ylo, :, cols] = turned[at + PT : at + 2 * PT]
            c_ref[ylo, 0, :, cols] = turned[at + 2 * PT : at + 3 * PT]


def flip(own, other):
    block = pl.BlockSpec((VB, 2 * FB), lambda x: (0, x))
    return pl.pallas_call(
        flip_kernel,
        grid=(4,),
        in_specs=[block, block],
        out_specs=[
            pl.BlockSpec((2, 1, PT, 2 * VB), lambda x: (0, x, 0, 0)),
            pl.BlockSpec((1, 2, PT, 2 * VB), lambda x: (x, 0, 0, 0)),
            pl.BlockSpec((2, 1, PT, 2 * VB), lambda x: (0, x, 0, 0)),
        ],
        out_shape=[
            jax.ShapeDtypeStruct((2, 4, PT, 2 * VB), BF),
            jax.ShapeDtypeStruct((4, 2, PT, 2 * VB), BF),
            jax.ShapeDtypeStruct((2, 4, PT, 2 * VB), BF),
        ],
        compiler_params=pltpu.CompilerParams(vmem_limit_bytes=VMEM),
        cost_estimate=pl.CostEstimate(
            flops=0, bytes_accessed=4 * VB * D * 2, transcendentals=0
        ),
        name="flip",
    )(own, other)


def act_kernel(tab, *refs):
    halves = [refs[2 * p : 2 * p + 2] for p in range(3)]
    own_ref, other_ref, tgt_ref = refs[6:9]
    expo_ref, bend_ref, rinv_ref, stat_ref, xt_out = refs[9:14]
    xt, squares, weights, acc, totals, stats, sems, out_sems, w_sems = refs[14:]
    step = pl.program_id(0)

    def fetch(src, tile, x, y, part):
        row = (x * 2 + (y & 1)) * FB + part * PT
        lanes = pl.ds(pl.multiple_of((y >> 1) * TB, TB), TB)
        pltpu.make_async_copy(
            src.at[pl.ds(0, PT)],
            xt.at[tile, pl.ds(pl.multiple_of(row, 16), PT), lanes],
            sems.at[tile],
        ).start()
        if part == 0:
            row = (x * 2 + (y & 1)) * SQ
            pltpu.make_async_copy(
                src.at[pl.ds(PT, SQ)],
                squares.at[tile, pl.ds(pl.multiple_of(row, 16), SQ), lanes],
                sems.at[tile],
            ).start()

    def issue(tile):
        for px in range(4):
            for py in range(4):
                x, y = at_of(tab, 0, px), at_of(tab, 1, py)
                places = (px, py, tile)
                fetch(halves[1][px >> 1].at[block_at(1, places)], tile, x, y, 1)
                fetch(halves[2][py >> 1].at[block_at(2, places)], tile, x, y, 2)
        for half in range(2):
            @pl.when((tile >> 1) == half)
            def _():
                for px in range(4):
                    for py in range(4):
                        fetch(
                            halves[0][half].at[block_at(0, (px, py, tile))],
                            tile, at_of(tab, 0, px), at_of(tab, 1, py), 0,
                        )

    def load(h, ref):
        return pltpu.make_async_copy(ref, weights.at[pl.ds(h * VB, VB)], w_sems.at[h])

    def arrived():
        pltpu.make_async_copy(xt.at[step], xt.at[step], sems.at[step]).wait()
        pltpu.make_async_copy(squares.at[step], squares.at[step], sems.at[step]).wait()
        pltpu.make_async_copy(xt.at[step], xt_out.at[step], out_sems.at[step]).start()

    @pl.when(step == 0)
    def _():
        load(0, own_ref).start()
        issue(step)
        load(1, other_ref).start()
        issue(step + 1)
        arrived()
        for h, ref in enumerate((own_ref, other_ref)):
            load(h, ref).wait()
            rows = pl.ds(h * VB, VB)
            acc[rows, :] = jnp.dot(weights[rows, :], xt[step], preferred_element_type=F32)

    @pl.when(step > 0)
    def _():
        @pl.when(step < 3)
        def _():
            issue(step + 1)

        arrived()
        acc[...] = jnp.dot(weights[...], xt[step], preferred_element_type=F32)

    mean = jnp.sum(squares[step].astype(F32), axis=0, keepdims=True) / D
    rinv = lax.rsqrt(mean + EPS)
    z = at_of(tab, 2, step)
    rinv_ref[z] = rinv
    tgt = tgt_ref[z]
    rows = 64
    zeros = jnp.zeros((8, 2 * TB), F32)
    sums = (zeros,) * 3
    inside = jnp.zeros((1, 2 * TB), jnp.bool_)

    def fold(v):
        return jnp.sum(v.reshape(rows // 8, 8, 2 * TB), axis=0)

    for h in range(2):
        row0 = lax.broadcasted_iota(jnp.int32, (rows, 2 * TB), 0) + tab[24 + h]
        inside = inside | ((tgt >= tab[24 + h]) & (tgt < tab[24 + h] + VB))

        def chunk(i, sums, h=h, row0=row0):
            total, slope, act_at = sums
            at = pl.multiple_of(i * rows, rows)
            here = pl.ds(h * VB + at, rows)
            act = acc[here, :] * rinv
            t = jnp.tanh(act * (1.0 / CAP))
            expo = jnp.exp(t * CAP)
            sharp = expo * (1.0 - t * t)
            expo_ref[0, here, :] = sharp
            return (
                total + fold(expo),
                slope + fold(sharp * act),
                act_at + fold(jnp.where(row0 + at == tgt, act, 0.0)),
            )

        sums = lax.fori_loop(0, VB // rows, chunk, sums)
    total, slope, act_at = [jnp.sum(s, axis=0, keepdims=True) for s in sums]
    t = jnp.tanh(act_at * (1.0 / CAP))
    bend = jnp.where(inside, 1.0 - t * t, 0.0)
    bend_ref[0] = bend
    sums = (total, t * CAP, slope, bend * act_at)
    for yhi in range(2):
        lanes = slice(yhi * TB, (yhi + 1) * TB)
        totals[pl.ds(z * 2 + yhi, 1), :] = sums[0][:, lanes]
        stats[yhi * 4 + z] = jnp.concatenate(
            [s[:, lanes] for s in sums[1:4]] + [jnp.zeros((5, TB), F32)], axis=0
        )

    @pl.when(step == 3)
    def _():
        for chip in range(64):
            stat_ref[chip, 0:8, :] = totals[...]
            stat_ref[chip, 8:16, :] = stats[chip % 8]
        for tile in range(4):
            pltpu.make_async_copy(xt.at[tile], xt_out.at[tile], out_sems.at[tile]).wait()


ANYWHERE = pl.BlockSpec(memory_space=pl.ANY)
SMEM_SPEC = pl.BlockSpec(memory_space=pltpu.SMEM)
VMEM_SPEC = pl.BlockSpec(memory_space=pltpu.VMEM)


def act_call(tab, halves, own, other, tgt):
    tile = pl.BlockSpec((1, 2 * VB, 2 * TB), lambda z, w: (z, 0, 0))
    rows = pl.BlockSpec((4, 1, 2 * TB), lambda z, w: (0, 0, 0))
    return pl.pallas_call(
        act_kernel,
        grid_spec=pltpu.PrefetchScalarGridSpec(
            num_scalar_prefetch=1,
            grid=(4,),
            in_specs=[ANYWHERE] * 8 + [rows],
            out_specs=[
                tile,
                pl.BlockSpec((1, 1, 2 * TB), lambda z, w: (z, 0, 0)),
                rows,
                pl.BlockSpec((64, 16, TB), lambda z, w: (0, 0, 0)),
                ANYWHERE,
            ],
            scratch_shapes=[
                pltpu.VMEM((4, D, 2 * TB), BF),
                pltpu.VMEM((4, 8 * SQ, 2 * TB), BF),
                pltpu.VMEM((2 * VB, D), BF),
                pltpu.VMEM((2 * VB, 2 * TB), F32),
                pltpu.VMEM((8, TB), F32),
                pltpu.VMEM((8, 8, TB), F32),
                pltpu.SemaphoreType.DMA((4,)),
                pltpu.SemaphoreType.DMA((4,)),
                pltpu.SemaphoreType.DMA((2,)),
            ],
        ),
        out_shape=[
            jax.ShapeDtypeStruct((4, 2 * VB, 2 * TB), F32),
            jax.ShapeDtypeStruct((4, 1, 2 * TB), F32),
            jax.ShapeDtypeStruct((4, 1, 2 * TB), F32),
            jax.ShapeDtypeStruct((64, 16, TB), F32),
            jax.ShapeDtypeStruct((4, D, 2 * TB), BF),
        ],
        compiler_params=pltpu.CompilerParams(vmem_limit_bytes=VMEM),
        cost_estimate=pl.CostEstimate(
            flops=2 * 1024 * 1024 * D, bytes_accessed=30_000_000, transcendentals=2 << 20
        ),
        name="act",
    )(tab, *halves, own, other, tgt)


def pieces(tab, lead, gz, gy, weights, outs, ready, done):
    w0, w1, w2 = weights
    out0, out1, out2 = outs
    ready(0)
    w = w0[...].reshape(8 * PT, 2 * VB)
    both = jnp.concatenate([gz[lead * 2], gz[lead * 2 + 1]], axis=1)
    got = jnp.dot(w, both, preferred_element_type=F32).astype(BF)
    for low in range(2):
        for x in range(4):
            for ylo in range(2):
                for yhi in range(2):
                    places = (place_of(tab, 0, x), place_of(tab, 1, yhi * 2 + ylo), lead * 2 + low)
                    row, lane = (ylo * 4 + x) * PT, (low * 2 + yhi) * TB
                    out0[block_at(0, places)] = got[row : row + PT, lane : lane + TB]
    done(0)
    ready(1)
    for low in range(2):
        place = lead * 2 + low
        x = at_of(tab, 0, place)
        w = w1[x].reshape(2 * PT, 2 * VB)
        tokens = jnp.concatenate([gz[z] for z in range(4)], axis=1)
        got = jnp.dot(w, tokens, preferred_element_type=F32).astype(BF)
        for z in range(4):
            for ylo in range(2):
                for yhi in range(2):
                    places = (place, place_of(tab, 1, yhi * 2 + ylo), z)
                    row, lane = ylo * PT, (z * 2 + yhi) * TB
                    out1[block_at(1, places)] = got[row : row + PT, lane : lane + TB]
    done(1)
    ready(2)
    for low in range(2):
        place = lead * 2 + low
        y = at_of(tab, 1, place)
        w = w2[y & 1].reshape(4 * PT, 2 * VB)
        tokens = jnp.concatenate([gy[y >> 1, pair] for pair in range(2)], axis=1)
        got = jnp.dot(w, tokens, preferred_element_type=F32).astype(BF)
        for x in range(4):
            for z in range(4):
                places = (place_of(tab, 0, x), place, z)
                out2[block_at(2, places)] = got[x * PT : (x + 1) * PT, z * TB : (z + 1) * TB]
    done(2)


def copies(pairs, sems):
    return [
        pltpu.make_async_copy(src, dst, sems.at[i]) for i, (src, dst) in enumerate(pairs)
    ]


def grad_kernel(tab, expo_ref, bend_ref, totals_ref, rinv_ref, tgt_ref, *refs):
    w_refs, out_refs = refs[:3], refs[3:10]
    expo, w0, w1, w2, gz, gr, gy, away0, away1, away2, in_sems, out_sems = refs[10:]
    weights, away = (w0, w1, w2), (away0, away1, away2)
    tiles = [(expo_ref.at[i], expo.at[i]) for i in range(4)]
    incoming = copies(tiles + list(zip(w_refs, weights)), in_sems)
    by_rows = (gr.at[:, pl.ds(0, VB)], gr.at[:, pl.ds(VB, VB)])
    outgoing = copies(list(zip(by_rows + (gz, gy) + away, out_refs)), out_sems)
    for copy in incoming:
        copy.start()
    rows = 128
    inv = 1.0 / jnp.sum(totals_ref[...], axis=0)[0:8]
    line = lax.broadcasted_iota(jnp.int32, (8, TB), 0)

    def chunk(i, carry, place, h, inv_z, rinv, bend, tgt, row0):
        at = pl.multiple_of(i * rows, rows)
        here = pl.ds(h * VB + at, rows)
        g = expo[place, here, :] * inv_z - jnp.where(row0 + at == tgt, bend, 0.0)
        gr[place, here, :] = (g * rinv).astype(BF)
        g = g.astype(BF)
        gz[place, here, :] = g
        for yhi in range(2):
            gy[yhi, place // 2, here, pl.ds(place % 2 * TB, TB)] = g[:, yhi * TB : (yhi + 1) * TB]
        return carry

    for place in range(4):
        z = at_of(tab, 2, place)
        inv_z = jnp.concatenate(
            [
                jnp.sum(jnp.where(line == z * 2 + yhi, inv, 0.0), axis=0, keepdims=True)
                for yhi in range(2)
            ],
            axis=1,
        )
        incoming[place].wait()
        for h in range(2):
            row0 = lax.broadcasted_iota(jnp.int32, (rows, 2 * TB), 0) + tab[24 + h]
            lax.fori_loop(
                0,
                VB // rows,
                functools.partial(
                    chunk, place=place, h=h, inv_z=inv_z, rinv=rinv_ref[z],
                    bend=bend_ref[place], tgt=tgt_ref[z], row0=row0,
                ),
                0,
            )
    for copy in outgoing[:4]:
        copy.start()
    pieces(
        tab, 1, gz, gy, weights, away,
        lambda p: incoming[4 + p].wait(), lambda p: outgoing[4 + p].start(),
    )
    for copy in outgoing:
        copy.wait()


def keep_kernel(tab, gz_ref, gy_ref, *refs):
    w_refs, out_refs = refs[:3], refs[3:6]
    gz, w0, w1, gy, w2, kept0, kept1, kept2, in_sems, out_sems = refs[6:]
    kept = (kept0, kept1, kept2)
    incoming = copies(
        [(gz_ref, gz), (w_refs[0], w0), (w_refs[1], w1), (gy_ref, gy), (w_refs[2], w2)], in_sems
    )
    outgoing = copies(list(zip(kept, out_refs)), out_sems)
    for copy in incoming:
        copy.start()

    def ready(p):
        for copy in ((0, 1), (2,), (3, 4))[p]:
            incoming[copy].wait()

    pieces(tab, 0, gz, gy, (w0, w1, w2), kept, ready, lambda p: outgoing[p].start())
    for copy in outgoing:
        copy.wait()


HALF = (32, PT, TB)
GZ = (4, 2 * VB, 2 * TB)
GR = (4, VB, 2 * TB)
GY = (2, 2, 2 * VB, 2 * TB)
W_SHAPES = ((2, 4, PT, 2 * VB), (4, 2, PT, 2 * VB), (2, 4, PT, 2 * VB))


def bf16_out(*shapes):
    return [jax.ShapeDtypeStruct(shape, BF) for shape in shapes]


def bf16_vmem(*shapes):
    return [pltpu.VMEM(shape, BF) for shape in shapes]


def grad_call(tab, expo, bend, totals, rinv, tgt, turned):
    return pl.pallas_call(
        grad_kernel,
        in_specs=[SMEM_SPEC, ANYWHERE] + [VMEM_SPEC] * 4 + [ANYWHERE] * 3,
        out_specs=[ANYWHERE] * 7,
        out_shape=bf16_out(GR, GR, GZ, GY, HALF, HALF, HALF),
        scratch_shapes=[pltpu.VMEM(GZ, F32)]
        + bf16_vmem(*W_SHAPES, GZ, GZ, GY, HALF, HALF, HALF)
        + [pltpu.SemaphoreType.DMA((7,)), pltpu.SemaphoreType.DMA((7,))],
        compiler_params=pltpu.CompilerParams(vmem_limit_bytes=VMEM),
        cost_estimate=pl.CostEstimate(
            flops=1024 * 1024 * D, bytes_accessed=24_000_000, transcendentals=0
        ),
        name="grad",
    )(tab, expo, bend, totals, rinv, tgt, *turned)


def keep_call(tab, gz, gy, turned):
    return pl.pallas_call(
        keep_kernel,
        in_specs=[SMEM_SPEC] + [ANYWHERE] * 5,
        out_specs=[ANYWHERE] * 3,
        out_shape=bf16_out(HALF, HALF, HALF),
        scratch_shapes=bf16_vmem(
            GZ, W_SHAPES[0], W_SHAPES[1], GY, W_SHAPES[2], HALF, HALF, HALF
        )
        + [pltpu.SemaphoreType.DMA((5,)), pltpu.SemaphoreType.DMA((3,))],
        compiler_params=pltpu.CompilerParams(vmem_limit_bytes=VMEM),
        cost_estimate=pl.CostEstimate(
            flops=1024 * D, bytes_accessed=1_000_000, transcendentals=0
        ),
        name="keep",
    )(tab, gz, gy, *turned)


def head_kernel(own_gr, twin_gr, own_xt, twin_xt, w, *refs):
    head_ref, gain_ref = refs[-2:]
    got = lax.dot_general(
        jnp.concatenate([gr[z] for gr in (own_gr, twin_gr) for z in range(4)], axis=1),
        jnp.concatenate([xt[z] for xt in (own_xt, twin_xt) for z in range(4)], axis=1),
        (((1,), (1,)), ((), ())), preferred_element_type=F32,
    )
    head_ref[...] = got.astype(BF)
    gain = jnp.sum(got * w[...].astype(F32), axis=0, keepdims=True)
    for i in range(gain_ref.shape[1]):
        gain_ref[0, i : i + 1, :] = gain[:, i * TB : (i + 1) * TB]


TILE = 768


def head_call(grs, xts, w, first, count, held=()):
    cols = pl.BlockSpec((VB, TILE), lambda f: (0, f + first))
    rows = pl.BlockSpec(GR, lambda f: (0, 0, 0), pipeline_mode=pl.Buffered(1))
    tokens = pl.BlockSpec((4, TILE, 2 * TB), lambda f: (0, f + first, 0))
    return pl.pallas_call(
        head_kernel,
        grid=(count,),
        in_specs=[rows, rows, tokens, tokens, cols] + [ANYWHERE] * len(held),
        out_specs=[cols, pl.BlockSpec((1, TILE // TB, TB), lambda f: (f, 0, 0))],
        out_shape=bf16_out((VB, D)) + [jax.ShapeDtypeStruct((count, TILE // TB, TB), F32)],
        input_output_aliases={5 + i: i for i in range(len(held))},
        compiler_params=pltpu.CompilerParams(vmem_limit_bytes=VMEM),
        cost_estimate=pl.CostEstimate(
            flops=1024 * D, bytes_accessed=1_000_000, transcendentals=0
        ),
        name="head",
    )(*grs, *xts, w, *held)


def sum_kernel(terms, *refs):
    ins, outs = refs[: 3 * terms], refs[3 * terms :]
    for p in range(3):
        blocks = [a[...] for a in ins[terms * p : terms * (p + 1)]]
        got = functools.reduce(lambda a, b: a + b, blocks)
        if len(outs) == 3:
            outs[p][...] = got
        else:
            outs[-1][:, p * PT : (p + 1) * PT, :] = got
    if len(outs) == 2:
        outs[-1][:, FB : FB + SQ, :] = outs[0][...]


def sum_call(here, count, gains=None):
    step = count // 2
    terms = len(here[0])
    specs = [
        pl.BlockSpec((step, PT, TB), lambda i, first=first // step: (i + first, 0, 0))
        for part in here
        for _, first in part
    ]
    arrays = [a for part in here for a, _ in part]
    if gains is None:
        out_specs = [pl.BlockSpec((step, PT, TB), lambda i: (i, 0, 0))] * 3
        out_shape = bf16_out(*[(count, PT, TB)] * 3)
    else:
        specs.append(pl.BlockSpec((step, SQ, TB), lambda i: (i, 0, 0)))
        arrays.append(gains)
        out_specs = pl.BlockSpec((step, FB + SQ, TB), lambda i: (i, 0, 0))
        out_shape = bf16_out((count, FB + SQ, TB))[0]
    return pl.pallas_call(
        functools.partial(sum_kernel, terms),
        grid=(count // step,),
        in_specs=specs,
        out_specs=out_specs,
        out_shape=out_shape,
        compiler_params=pltpu.CompilerParams(vmem_limit_bytes=VMEM),
        cost_estimate=pl.CostEstimate(flops=4 << 20, bytes_accessed=6_000_000, transcendentals=0),
        name="sum%d" % terms,
    )(*arrays)


def shards(section_output, norm_gain, head_weight, targets):
    x, ylo, yhi, z, core = (lax.axis_index(a) for a in AX)
    y = yhi * 2 + ylo
    shard = (((x * 2 + ylo) * 2 + yhi) * 4 + z) * 2 + core
    tab = table(x, y, z, core, shard)

    xt = section_output.T.astype(F32)
    gain = norm_gain.astype(F32)[:, None]
    scaled_x = (xt * gain).astype(BF)
    squares = jnp.sum(xt * xt, axis=0, keepdims=True)
    extra = jnp.concatenate(
        split3(squares) + [jnp.zeros((SQ - 3, TB), BF)], axis=0
    )
    block = jnp.concatenate([scaled_x[:PT], extra, scaled_x[PT:]], axis=0)
    other = send(head_weight, TWIN)
    turned = flip(head_weight, other)

    tgt = lax.dynamic_index_in_dim(
        targets.reshape(2, 4, 2, TB), core, axis=2, keepdims=False
    ).transpose(1, 0, 2).reshape(4, 1, 2 * TB)
    halves = gather(block)
    owner = jnp.stack([tab[ex] * 2 + (tab[4 + ey] & 1) for ex, ey, _ in BITS])
    owner = (owner[:, None, None] == jnp.arange(8, dtype=jnp.int32)[None, :, None]).astype(F32)
    halves, turned, tgt, tab, owner = lax.optimization_barrier((halves, turned, tgt, tab, owner))

    expo, bend, rinv, stats, xt_all = act_call(tab, halves, head_weight, other, tgt)
    stats = lax.all_to_all(stats, AX[:4], 0, 0)
    stats, xt_all = lax.optimization_barrier((stats, xt_all))
    xts = (xt_all, send(xt_all, TWIN))

    own_gr, other_gr, gz, gy, *away = grad_call(tab, expo, bend, stats, rinv, tgt, turned)

    bound = lax.optimization_barrier

    def exchange(away, phase):
        return [send(away[p], across(ORDER[p][phase])) for p in range(3)]

    got1 = exchange(away, 2)
    grs = (own_gr, send(other_gr, TWIN))
    kept = keep_call(tab, gz, gy, turned)
    kept, grs = bound((kept, grs))
    head_grad, gain0 = head_call(grs, xts, head_weight, 0, 4)
    got1, kept, grs, head_grad, gain0 = bound((got1, kept, grs, head_grad, gain0))
    away = sum_call([[(kept[p], 16), (got1[p], 16)] for p in range(3)], 16)

    away, grs, head_grad = bound((away, grs, head_grad))
    got2 = exchange(away, 1)
    head_grad, gain1 = head_call(grs, xts, head_weight, 4, 2, (head_grad,))
    gains = jnp.concatenate([gain0, gain1])
    gains = gains + send(gains, across(1))
    got2, gains = bound((got2, gains))
    more = send(gains, across(0))
    away = sum_call([[(kept[p], 8), (got1[p], 8), (got2[p], 8)] for p in range(3)], 8)

    away, more, gains = bound((away, more, gains))
    got3 = exchange(away, 0)
    gains = gains + more
    more = send(gains, across(2))
    got3, more = bound((got3, more))
    gains = gains + more
    here = [[(a[p], 0) for a in (kept, got1, got2, got3)] for p in range(3)]

    gains = jnp.sum(owner * gains.reshape(1, 8, FB), axis=1)
    gains = jnp.concatenate([gains, jnp.zeros((8, 5 * TB - FB), F32)], axis=1)
    gains = jnp.stack(split3(gains) + [jnp.zeros((8, 5 * TB), BF)], axis=1)
    gains = gains.reshape(8, 20, TB)[:, :SQ]

    blocks = in_cube(sum_call(here, 8, gains))
    blocks = jnp.sum(blocks.astype(F32), axis=0)
    grad_hidden = blocks[:FB]
    gains = jnp.sum(blocks[FB : FB + 15].reshape(3, 5 * TB), axis=0)[:FB]
    gain_grad = (gains + send(gains, TWIN)) / norm_gain.astype(F32)

    row = jnp.sum(stats, axis=0)
    picked, slope, slope_at = row[8:9], row[9:10], row[10:11]
    sum_exp = lax.dynamic_slice(row, (z * 2 + yhi, 0), (1, TB))
    rinv = lax.dynamic_slice(rinv, (z, 0, yhi * TB), (1, 1, TB)).reshape(1, TB)
    token_loss = (jnp.log(sum_exp) - picked).reshape(TB)
    inner = slope / sum_exp - slope_at
    grad_input = (rinv * (grad_hidden * gain) - xt * (rinv * rinv * inner / D)).astype(BF).T
    return (token_loss, grad_input, head_grad, gain_grad)


def solution(mesh):
    fine = Mesh(mesh.devices.reshape(4, 2, 2, 4, 2), AX)
    pipe, dp = ("x", "ylo"), ("yhi", "z", "core")
    return jax.shard_map(
        shards,
        mesh=fine,
        in_specs=(P(dp, pipe), P(pipe), P(pipe + dp, None), P()),
        out_specs=(P(dp), P(dp, pipe), P(pipe + dp, None), P(pipe)),
        check_vma=False,
    )
```
